32 devices in a mesh: groups: 2 (over y), ctx: 4 (over z), head: 2 (over x), rep: 2 (over core).
Axes of the slice: x: 2, y: 2, z: 4, core: 2. Of those that a mesh axis runs over, the one named last changes fastest.
Arguments:
- queries: bfloat16 [1024, 5120], P(('groups', 'ctx'), 'head'), parts along dimension 0, may hold values from -50 to 50
- key_vectors: bfloat16 [1024, 5120], P(('groups', 'ctx'), 'head'), parts along dimension 0, may hold values from -5 to 5
- values: bfloat16 [1024, 5120], P(('groups', 'ctx'), 'head'), parts along dimension 0, may hold values from -6 to 6
- learn_rates: float32 [8, 1024], P('head', ('groups', 'ctx')), parts along dimension 1, may hold values from 0.02 to 0.2
- fast_weights: float32 [16, 3, 640, 640], P(('groups', 'head'), None, ('ctx', 'rep')), parts along dimension 0, may hold values from -0.25 to 0.25
- momentum: float32 [16, 3, 640, 640], P(('groups', 'head'), None, ('ctx', 'rep')), parts along dimension 0, may hold values from -0.25 to 0.25
Outputs:
- layer_output: bfloat16 [1024, 5120], P(('groups', 'ctx'), ('head', 'rep')), parts along dimension 0
- fast_updated: float32 [16, 3, 640, 640], P(('groups', 'head'), None, ('ctx', 'rep')), parts along dimension 0
The draws below stay inside these ranges and needn't reach their ends.
There are 2 independent parts, one for each index of `groups`. The reference program is written for one: setup_inputs(seed, part) draws one part's arguments, and reference() takes and returns one part's arrays. A program takes and returns all parts, laid end to end along the dimension named above; each array names one. Nothing has to cross between parts.
All inputs are finite; a program needn't handle non-finite values.
Results may differ from the reference program's by a relative error of at most 0.038.
Values may be sent and summed in bfloat16 or wider, within the bound.
A program may use at most 64 MiB of HBM per device.

```python
import math
import jax
import jax.numpy as jnp
from jax import lax

HEADS = 8
DH = 640
TOK_DEV = 128
TOKENS = 512
N_CTX = 4


def drawn_pair(key):
    key_keys = jax.random.fold_in(key, 101)
    key_queries = jax.random.fold_in(key, 202)
    base_keys = jnp.clip(jax.random.normal(key_keys, (TOKENS, HEADS * DH), jnp.float32), -5.0, 5.0)
    base_queries = jnp.clip(jax.random.normal(key_queries, (TOKENS, HEADS * DH), jnp.float32), -5.0, 5.0)
    return (base_queries, base_keys)


def draw_queries(key, part):
    return drawn_pair(key)[0].astype(jnp.bfloat16)


def draw_key_vectors(key, part):
    return drawn_pair(key)[1].astype(jnp.bfloat16)


def level_of(rng, dims, pieces, smallest, high):
    factor_of, own = 1.0, jax.random.fold_in(rng, 6)
    for axis_at, blocks in pieces:
        heights = jnp.exp(jax.random.uniform(jax.random.fold_in(own, axis_at), (blocks,), jnp.float32, smallest / len(pieces), high / len(pieces)))
        factor_of = factor_of * jnp.repeat(heights, dims[axis_at] // blocks).reshape([-1 if axis == axis_at else 1 for axis in range(len(dims))])
    return factor_of


def noise(rng, shape, spread, most, cuts=(), kind=jnp.bfloat16):
    result = jax.random.normal(rng, shape, jnp.float32) * spread
    if len(cuts) > 0:
        result = level_of(rng, shape, cuts, -0.22, 0.18) * result
    return jnp.clip(result, min=-most, max=most).astype(kind)


def setup_inputs(seed: int = 0, part: int = 0) -> dict:
    key_list = jax.random.split(jax.random.key(seed), 7)
    own_keys = jax.random.split(jax.random.fold_in(key_list[6], part), 7)
    return {
        "queries": draw_queries(jax.random.fold_in(jax.random.fold_in(key_list[6], part), 71), part),
        "key_vectors": draw_key_vectors(jax.random.fold_in(jax.random.fold_in(key_list[6], part), 71), part),
        "values": noise(own_keys[2], (TOKENS, HEADS * DH), 1.0, 6.0, ((0, 4), (1, 2))),
        "learn_rates": jnp.clip(jnp.exp(math.log(0.2) - 2.3025851 * jax.random.uniform(own_keys[3], (HEADS, TOKENS), jnp.float32) ** level_of(own_keys[3], (HEADS, TOKENS), ((0, 2), (1, 4)), -0.2, 0.2)), 0.02, 0.2),
        "fast_weights": noise(own_keys[4], (HEADS, 3, DH, DH), DH ** -0.5, 0.25, ((0, 2), (2, 8)), jnp.float32),
        "momentum": noise(own_keys[5], (HEADS, 3, DH, DH), DH ** -0.5, 0.25, ((0, 2), (2, 8)), jnp.float32),
    }


epsilon = 1e-06
momentum_decay = 0.9

def unit_rows(tensor):
    widened = tensor.astype(jnp.float32)
    factor = lax.rsqrt(lax.optimization_barrier(jnp.mean(widened * widened, axis=-1, keepdims=True)) + epsilon)
    return (widened * factor).astype(jnp.bfloat16)

def block_sum(left, right):
    left_blocks = left.reshape(N_CTX, TOK_DEV, -1).astype(jnp.float32)
    right_blocks = right.reshape(N_CTX, TOK_DEV, -1).astype(jnp.float32)
    partial_sums = jnp.einsum('btr,btd->brd', left_blocks, right_blocks)
    rounded = lax.optimization_barrier(partial_sums.astype(jnp.bfloat16))
    return lax.optimization_barrier(jnp.sum(rounded.astype(jnp.float32), axis=0))

def head_gradient(operands):
    key_head, cot_head, weights = operands
    gate = jnp.dot(key_head, weights[0].T, preferred_element_type=jnp.float32)
    upward = jnp.dot(key_head, weights[1].T, preferred_element_type=jnp.float32)
    back = jnp.dot(cot_head, weights[2].T, preferred_element_type=jnp.float32)
    sigma = jax.nn.sigmoid(gate)
    activated = jax.nn.silu(gate)
    hidden = (activated * upward).astype(jnp.bfloat16)
    gate_back = (back * upward * sigma * (1.0 + gate * (1.0 - sigma))).astype(jnp.bfloat16)
    up_back = (back * activated).astype(jnp.bfloat16)
    return jnp.stack([block_sum(gate_back, key_head), block_sum(up_back, key_head), block_sum(hidden, cot_head)])

def head_apply(operands):
    query_head, weights = operands
    gate = jnp.dot(query_head, weights[0].T, preferred_element_type=jnp.float32)
    upward = jnp.dot(query_head, weights[1].T, preferred_element_type=jnp.float32)
    hidden = (jax.nn.silu(gate) * upward).astype(jnp.bfloat16)
    return jnp.dot(hidden, weights[2], preferred_element_type=jnp.float32)

def head_attention(operands):
    query_head, key_head, value_head = operands
    query_blocks = query_head.reshape(N_CTX, TOK_DEV, DH).astype(jnp.float32)
    key_blocks = key_head.reshape(N_CTX, TOK_DEV, DH).astype(jnp.float32)
    value_blocks = value_head.reshape(N_CTX, TOK_DEV, DH).astype(jnp.float32)
    zero_block = jnp.zeros((1, TOK_DEV, DH), jnp.float32)
    key_window = jnp.concatenate([jnp.concatenate([zero_block, key_blocks[:-1]], axis=0), key_blocks], axis=1)
    value_window = jnp.concatenate([jnp.concatenate([zero_block, value_blocks[:-1]], axis=0), value_blocks], axis=1)
    scores = jnp.einsum('btd,bsd->bts', query_blocks, key_window) * DH ** (-0.5)
    block_index = jnp.arange(N_CTX)[:, None, None]
    position = jnp.arange(2 * TOK_DEV)[None, None, :]
    valid = jnp.logical_or(block_index > 0, position >= TOK_DEV)
    scores = jnp.where(valid, scores, -jnp.inf)
    peak = lax.optimization_barrier(jnp.max(scores, axis=-1, keepdims=True))
    weights = jnp.exp(scores - peak)
    probs = (weights / lax.optimization_barrier(jnp.sum(weights, axis=-1, keepdims=True))).astype(jnp.bfloat16)
    attended = jnp.einsum('bts,bsd->btd', probs.astype(jnp.float32), value_window)
    return attended.reshape(TOKENS, DH)

def reference(queries, key_vectors, values, learn_rates, fast_weights, momentum):
    query_heads = queries.reshape(TOKENS, HEADS, DH)
    key_heads = key_vectors.reshape(TOKENS, HEADS, DH)
    value_heads = values.reshape(TOKENS, HEADS, DH)
    query_unit = unit_rows(query_heads)
    key_unit = unit_rows(key_heads)
    token_scale = float(TOKENS) ** (-0.5)
    cotangent = (-(learn_rates.T[:, :, None] * token_scale) * value_heads.astype(jnp.float32)).astype(jnp.bfloat16)
    weights_low = fast_weights.astype(jnp.bfloat16)
    gradient = lax.map(head_gradient, (jnp.transpose(key_unit, (1, 0, 2)), jnp.transpose(cotangent, (1, 0, 2)), weights_low))
    fast_updated = fast_weights - (momentum_decay * momentum + gradient)
    new_low = fast_updated.astype(jnp.bfloat16)
    fast_out = lax.map(head_apply, (jnp.transpose(query_unit, (1, 0, 2)), new_low))
    attended = lax.map(head_attention, (jnp.transpose(query_heads, (1, 0, 2)), jnp.transpose(key_heads, (1, 0, 2)), jnp.transpose(value_heads, (1, 0, 2))))
    combined = jnp.transpose(attended + fast_out, (1, 0, 2))
    layer_output = combined.astype(jnp.bfloat16).reshape(TOKENS, HEADS * DH)
    return (layer_output, fast_updated)
```

```python
import functools

import jax
import jax.numpy as jnp
from jax import lax
from jax.experimental import pallas as pl
from jax.experimental.pallas import tpu as pltpu
from jax.sharding import PartitionSpec as P

epsilon = 1e-06
momentum_decay = 0.9


def passed_along(value, axis, steps):
    count = lax.axis_size(axis)
    initial, last = (max(0, -steps), min(count, count - steps))
    return lax.ppermute(value, axis, [(source, source + steps) for source in range(initial, last)])


def unit_rows(tensor):
    widened = tensor.astype(jnp.float32)
    factor = lax.rsqrt(jnp.mean(widened * widened, axis=-1, keepdims=True) + epsilon)
    return (widened * factor).astype(jnp.bfloat16)


def swiglu_apply(inputs, weights):
    gate = jnp.einsum("thd,hrd->htr", inputs, weights[:, 0], preferred_element_type=jnp.float32)
    upward = jnp.einsum("thd,hrd->htr", inputs, weights[:, 1], preferred_element_type=jnp.float32)
    hidden = (jax.nn.silu(gate) * upward).astype(jnp.bfloat16)
    return jnp.einsum("htr,hrd->htd", hidden, weights[:, 2], preferred_element_type=jnp.float32)


def window_attention(query_own, key_own, value_own, key_prior, value_prior, first_block):
    tok_rows = query_own.shape[0]
    per_rep = query_own.shape[1]
    width = query_own.shape[2]
    block_rows = min(tok_rows, 512)
    block_count = tok_rows // block_rows
    key_window = jnp.concatenate([key_prior, key_own], axis=0)
    value_window = jnp.concatenate([value_prior, value_own], axis=0)
    score_scale = width ** (-0.5)
    position = jnp.arange(2 * tok_rows)
    valid = jnp.logical_or(position >= tok_rows, jnp.logical_not(first_block))
    query_blocks = query_own.reshape(block_count, block_rows, per_rep, width)

    def one_block(query_block):
        scores = (
            jnp.einsum("tad,sad->ats", query_block, key_window, preferred_element_type=jnp.float32)
            * score_scale
        )
        scores = jnp.where(valid[None, None, :], scores, -jnp.inf)
        peak = jnp.max(scores, axis=-1, keepdims=True)
        weights = jnp.exp(scores - peak)
        probs = (weights / jnp.sum(weights, axis=-1, keepdims=True)).astype(jnp.bfloat16)
        return jnp.einsum("ats,sad->tad", probs, value_window, preferred_element_type=jnp.float32)

    return lax.map(one_block, query_blocks).reshape(tok_rows, per_rep, width)


def on_device(queries, key_vectors, values, learn_rates, fast_weights, momentum):
    tok_rows = queries.shape[0]
    head_count = fast_weights.shape[0]
    width = fast_weights.shape[3]
    rep_count = lax.axis_size("rep")
    per_rep = head_count // rep_count
    rep_index = lax.axis_index("rep")
    ctx_index = lax.axis_index("ctx")
    total_tokens = tok_rows * lax.axis_size("ctx")
    query_heads = queries.reshape(tok_rows, head_count, width)
    key_heads = key_vectors.reshape(tok_rows, head_count, width)
    value_heads = values.reshape(tok_rows, head_count, width)
    query_unit = unit_rows(query_heads)
    key_unit = unit_rows(key_heads)
    token_scale = float(total_tokens) ** (-0.5)
    cotangent = (
        -(learn_rates.T[:, :, None] * token_scale) * value_heads.astype(jnp.float32)
    ).astype(jnp.bfloat16)
    weight_rows = lax.all_gather(fast_weights.astype(jnp.bfloat16), "ctx", axis=2, tiled=True)
    gate = jnp.einsum(
        "thd,hrd->htr", key_unit, weight_rows[:, 0], preferred_element_type=jnp.float32
    )
    upward = jnp.einsum(
        "thd,hrd->htr", key_unit, weight_rows[:, 1], preferred_element_type=jnp.float32
    )
    back = jnp.einsum(
        "thd,hrd->htr", cotangent, weight_rows[:, 2], preferred_element_type=jnp.float32
    )
    sigma = jax.nn.sigmoid(gate)
    activated = jax.nn.silu(gate)
    hidden = (activated * upward).astype(jnp.bfloat16)
    gate_back = (back * upward * sigma * (1.0 + gate * (1.0 - sigma))).astype(jnp.bfloat16)
    up_back = (back * activated).astype(jnp.bfloat16)
    grad_gate = jnp.einsum("htr,thd->hrd", gate_back, key_unit, preferred_element_type=jnp.float32)
    grad_up = jnp.einsum("htr,thd->hrd", up_back, key_unit, preferred_element_type=jnp.float32)
    grad_down = jnp.einsum("htr,thd->hrd", hidden, cotangent, preferred_element_type=jnp.float32)
    gradient = jnp.stack([grad_gate, grad_up, grad_down], axis=1)
    share = lax.psum_scatter(
        gradient.astype(jnp.bfloat16), "ctx", scatter_dimension=2, tiled=True
    ).astype(jnp.float32)
    fast_updated = fast_weights - (momentum_decay * momentum + share)
    new_rows = lax.all_gather(fast_updated.astype(jnp.bfloat16), "ctx", axis=2, tiled=True)
    own_start = rep_index * per_rep
    partial_out = swiglu_apply(query_unit, new_rows)
    traded = lax.all_to_all(
        partial_out.astype(jnp.bfloat16), "rep", split_axis=0, concat_axis=0, tiled=True
    ).astype(partial_out.dtype)
    fast_out = jnp.sum(traded.reshape(rep_count, per_rep, tok_rows, width), axis=0)
    attend_query = lax.dynamic_slice_in_dim(query_heads, own_start, per_rep, 1)
    attend_key = lax.dynamic_slice_in_dim(key_heads, own_start, per_rep, 1)
    attend_value = lax.dynamic_slice_in_dim(value_heads, own_start, per_rep, 1)
    key_prior, value_prior = passed_along((attend_key, attend_value), "ctx", 1)
    attended = window_attention(
        attend_query, attend_key, attend_value, key_prior, value_prior, ctx_index == 0
    )
    combined = attended + jnp.transpose(fast_out, (1, 0, 2))
    layer_output = combined.astype(jnp.bfloat16).reshape(tok_rows, per_rep * width)
    return (layer_output, fast_updated)


def contract(left, right, left_dim, right_dim):
    return lax.dot_general(
        left, right, (((left_dim,), (right_dim,)), ((), ())), preferred_element_type=jnp.float32
    )


def fused_kernel(
    n, mine, decay, token_scale,
    q_hbm, k_hbm, v_hbm, lr_ref, fw_hbm, mom_hbm,
    out_hbm, fast_hbm,
    tok, lrs, fw, mom, weights, w_send, base_peer, base_send, grad, new_w, g_send, g_recv,
    attn, part, sums_right, sums_left, out_v,
    in_sem, tok_send, tok_recv, lr_send, lr_recv, pair_send, pair_recv, sum_send, sum_recv, out_sem,
):
    MESH = pl.DeviceIdType.MESH
    z = lax.axis_index("ctx")
    r = lax.axis_index("rep")
    heads, _, rows, width = fw.shape
    tokens = tok.shape[3]
    has_left, has_right = z > 0, z < n - 1
    own, other = r * mine, (1 - r) * mine

    def load(c, h):
        ref = (k_hbm, v_hbm, q_hbm)[c]
        column = pl.multiple_of((own + h) * width, 128)
        return pltpu.make_async_copy(ref.at[:, pl.ds(column, width)], tok.at[z, c, h], in_sem.at[c, h])

    for c in range(3):
        for h in range(mine):
            load(c, h).start()
    load_fw = pltpu.make_async_copy(fw_hbm, fw, in_sem.at[3, 0])
    load_mom = pltpu.make_async_copy(mom_hbm, mom, in_sem.at[3, 1])
    load_fw.start()
    load_mom.start()
    for i in range(heads):
        lrs[z, i] = lr_ref[i : i + 1, :] * (-token_scale)

    barrier = pltpu.get_barrier_semaphore()
    pl.semaphore_signal(barrier, inc=1, device_id={"rep": 1 - r}, device_id_type=MESH)

    @pl.when(has_left)
    def _():
        pl.semaphore_signal(barrier, inc=1, device_id={"ctx": z - 1}, device_id_type=MESH)

    @pl.when(has_right)
    def _():
        pl.semaphore_signal(barrier, inc=1, device_id={"ctx": z + 1}, device_id_type=MESH)

    pl.semaphore_wait(barrier, 1 + has_left.astype(jnp.int32) + has_right.astype(jnp.int32))

    def tok_copy(b, c, h, way):
        return pltpu.make_async_remote_copy(
            src_ref=tok.at[b, c, h], dst_ref=tok.at[b, c, h],
            send_sem=tok_send.at[way, b, c, h], recv_sem=tok_recv.at[b, c, h],
            device_id={"ctx": z + 1 - 2 * way}, device_id_type=MESH,
        )

    def lr_copy(b, way):
        return pltpu.make_async_remote_copy(
            src_ref=lrs.at[b], dst_ref=lrs.at[b],
            send_sem=lr_send.at[way, b], recv_sem=lr_recv.at[b],
            device_id={"ctx": z + 1 - 2 * way}, device_id_type=MESH,
        )

    def pair_copy(which):
        src, dst = (
            (w_send, weights.at[:, :, pl.ds(rows, rows), :]),
            (base_send, base_peer),
            (g_send, g_recv),
        )[which]
        return pltpu.make_async_remote_copy(
            src_ref=src, dst_ref=dst, send_sem=pair_send.at[which], recv_sem=pair_recv.at[which],
            device_id={"rep": 1 - r}, device_id_type=MESH,
        )

    def sum_copy(b, h, way):
        return pltpu.make_async_remote_copy(
            src_ref=part.at[b, h], dst_ref=(sums_right, sums_left)[way].at[b, h],
            send_sem=sum_send.at[b, h], recv_sem=sum_recv.at[way, b, h],
            device_id={"ctx": z + 1 - 2 * way}, device_id_type=MESH,
        )

    open_way = (has_right, has_left)

    def own_send(make):
        for way in range(2):
            pl.when(open_way[way])(lambda way=way: make(way).start())

    own_send(lambda way: lr_copy(z, way))
    for h in range(mine):
        for c in range(2):
            load(c, h).wait()
            own_send(lambda way: tok_copy(z, c, h, way))
    for h in range(mine):
        load(2, h).wait()

    def own_queries(step):
        for way in range(2):
            last = z if way == 0 else n - 1 - z

            @pl.when(jnp.logical_and(step == last, open_way[way]))
            def _(way=way):
                for h in range(mine):
                    tok_copy(z, 2, h, way).start()

    own_queries(0)

    load_fw.wait()
    for h in range(mine):
        for m in range(3):
            w_send[h, m] = fw[other + h, m].astype(jnp.bfloat16)
    pair_copy(0).start()
    for h in range(mine):
        for m in range(3):
            weights[h, m, :rows] = fw[own + h, m].astype(jnp.bfloat16)
    load_mom.wait()
    for h in range(mine):
        for m in range(3):
            base_send[h, m] = fw[other + h, m] - decay * mom[other + h, m]
    pair_copy(1).start()
    pair_copy(0).wait_recv()

    def grad_block(b, first):
        @pl.loop(0, mine)
        def _(h):
            key = unit_rows(tok[b, 0, h])
            value = tok[b, 1, h]
            rate = lrs[b, own + h]
            both = contract(weights[h, 0:2].reshape(4 * rows, width), key, 1, 1)
            gate, upward = both[: 2 * rows], both[2 * rows :]
            back = contract(weights[h, 2], value, 1, 1) * rate
            sigma = jax.nn.sigmoid(gate)
            activated = gate * sigma
            hidden = (activated * upward * rate).astype(jnp.bfloat16)
            gate_back = (back * upward * sigma * (1.0 + gate * (1.0 - sigma))).astype(jnp.bfloat16)
            up_back = (back * activated).astype(jnp.bfloat16)
            terms = (
                contract(gate_back, key, 1, 0),
                contract(up_back, key, 1, 0),
                contract(hidden, value, 1, 0),
            )
            for m in range(3):
                grad[h, m] = terms[m] if first else grad[h, m] + terms[m]

    def attend(with_prior):
        @pl.loop(0, mine)
        def _(h):
            query = tok[z, 2, h]
            scale = width ** (-0.5)
            scores = contract(query, tok[z, 0, h], 1, 1) * scale
            peak = jnp.max(scores, axis=-1, keepdims=True)
            if with_prior:
                prior = contract(query, tok[z - 1, 0, h], 1, 1) * scale
                peak = jnp.maximum(peak, jnp.max(prior, axis=-1, keepdims=True))
                prior = jnp.exp(prior - peak)
            scores = jnp.exp(scores - peak)
            total = jnp.sum(scores, axis=-1, keepdims=True)
            if with_prior:
                total = total + jnp.sum(prior, axis=-1, keepdims=True)
            result = contract((scores / total).astype(jnp.bfloat16), tok[z, 1, h], 1, 0)
            if with_prior:
                result = result + contract((prior / total).astype(jnp.bfloat16), tok[z - 1, 1, h], 1, 0)
            attn[h] = result

    def from_left(step):
        return z - step >= 0

    def from_right(step):
        return z + step < n

    grad_block(z, True)

    @pl.when(z == 0)
    def _():
        attend(False)

    def pass_on(step, pieces, with_lr):
        arrives = (from_left(step), from_right(step))
        for way in range(2):
            b = z - step if way == 0 else z + step
            if with_lr:
                @pl.when(arrives[way])
                def _(way=way, b=b):
                    lr_copy(b, way).wait_recv()
                    pl.when(open_way[way])(lambda: lr_copy(b, way).start())

        for c, h in pieces:
            for way in range(2):
                b = z - step if way == 0 else z + step

                @pl.when(arrives[way])
                def _(way=way, b=b):
                    tok_copy(b, c, h, way).wait_recv()
                    pl.when(open_way[way])(lambda: tok_copy(b, c, h, way).start())

    def keys_step(step, carry):
        pass_on(step, [(c, h) for h in range(mine) for c in range(2)], True)
        own_queries(step)

        @pl.when(from_left(step))
        def _():
            grad_block(z - step, False)

        @pl.when(from_right(step))
        def _():
            grad_block(z + step, False)

        @pl.when(jnp.logical_and(step == 1, has_left))
        def _():
            attend(True)

        return carry

    lax.fori_loop(1, n, keys_step, 0)

    pair_copy(1).wait_recv()
    for h in range(mine):
        for m in range(3):
            fresh = fw[own + h, m] - (decay * mom[own + h, m] + grad[h, m, :rows])
            fw[own + h, m] = fresh
            new_w[h, m, :rows] = fresh.astype(jnp.bfloat16)
            new_w[h, m, rows:] = (base_peer[h, m] - grad[h, m, rows:]).astype(jnp.bfloat16)
            g_send[h, m] = grad[h, m, rows:].astype(jnp.bfloat16)
    pair_copy(2).start()
    store_own = pltpu.make_async_copy(
        fw.at[pl.ds(own, mine)], fast_hbm.at[pl.ds(own, mine)], out_sem.at[0]
    )
    store_own.start()

    def apply(b, h):
        query = unit_rows(tok[b, 2, h])
        gate = contract(query, new_w[h, 0], 1, 1)
        upward = contract(query, new_w[h, 1], 1, 1)
        hidden = (gate * jax.nn.sigmoid(gate) * upward).astype(jnp.bfloat16)
        return contract(hidden, new_w[h, 2], 1, 0)

    @pl.loop(0, mine)
    def _(h):
        attn[h] = attn[h] + apply(z, h)

    def queries_step(step, carry):
        pass_on(step, [(2, h) for h in range(mine)], False)
        for way in range(2):
            b = z - step if way == 1 else z + step
            source_there = from_left(step) if way == 1 else from_right(step)
            starts_here = jnp.logical_not(has_right if way == 1 else has_left)

            @pl.when(source_there)
            def _(b=b, way=way, starts_here=starts_here):
                @pl.loop(0, mine)
                def _(h):
                    part[b, h] = apply(b, h).astype(jnp.bfloat16)
                    pl.when(starts_here)(lambda: sum_copy(b, h, way).start())

        return carry

    lax.fori_loop(1, n, queries_step, 0)

    near_left = 2 * z < n - 1

    def merge_step(step, carry):
        for h in range(mine):
            for way, turn in ((0, near_left), (1, None), (0, jnp.logical_not(near_left))):
                b = step if way == 0 else n - 1 - step
                there = jnp.logical_and(b > z, has_left) if way == 0 else jnp.logical_and(b < z, has_right)

                @pl.when(there if turn is None else jnp.logical_and(there, turn))
                def _(b=b, way=way):
                    sum_copy(b, h, way).wait_recv()
                    arrived = (sums_right, sums_left)[way][b, h].astype(jnp.float32)
                    part[b, h] = (part[b, h].astype(jnp.float32) + arrived).astype(jnp.bfloat16)
                    sum_copy(b, h, way).start()

        return carry

    lax.fori_loop(1, n, merge_step, 0)

    pair_copy(2).wait_recv()
    for h in range(mine):
        for m in range(3):
            fw[other + h, m] = fw[other + h, m] - (
                decay * mom[other + h, m] + g_recv[h, m].astype(jnp.float32)
            )
    store_other = pltpu.make_async_copy(
        fw.at[pl.ds(other, mine)], fast_hbm.at[pl.ds(other, mine)], out_sem.at[1]
    )
    store_other.start()

    for h in range(mine):
        @pl.when(has_left)
        def _():
            sum_copy(z, h, 0).wait_recv()
            attn[h] = attn[h] + sums_right[z, h].astype(jnp.float32)

        @pl.when(has_right)
        def _():
            sum_copy(z, h, 1).wait_recv()
            attn[h] = attn[h] + sums_left[z, h].astype(jnp.float32)

        out_v[:, h * width : (h + 1) * width] = attn[h].astype(jnp.bfloat16)
    store_out = pltpu.make_async_copy(out_v, out_hbm, out_sem.at[2])
    store_out.start()

    for way in range(2):
        @pl.when(open_way[way])
        def _(way=way):
            lr_copy(z, way).wait_send()
            for h in range(mine):
                for c in range(3):
                    tok_copy(z, c, h, way).wait_send()

    def drain(step, carry):
        for way in range(2):
            b = z - step if way == 0 else z + step
            arrives = from_left(step) if way == 0 else from_right(step)

            @pl.when(jnp.logical_and(arrives, open_way[way]))
            def _(way=way, b=b):
                lr_copy(b, way).wait_send()
                for h in range(mine):
                    for c in range(3):
                        tok_copy(b, c, h, way).wait_send()

            @pl.when(arrives)
            def _(way=way, b=b):
                for h in range(mine):
                    sum_copy(b, h, 1 - way).wait_send()

        return carry

    lax.fori_loop(1, n, drain, 0)
    for which in range(3):
        pair_copy(which).wait_send()
    store_own.wait()
    store_other.wait()
    store_out.wait()


def fused_device(queries, key_vectors, values, learn_rates, fast_weights, momentum):
    n = lax.axis_size("ctx")
    tokens = queries.shape[0]
    heads, _, rows, width = fast_weights.shape
    mine = heads // 2
    bf16, f32 = jnp.bfloat16, jnp.float32
    hbm = pl.BlockSpec(memory_space=pl.ANY)
    dma = pltpu.SemaphoreType.DMA
    vmem = pltpu.VMEM
    return pl.pallas_call(
        functools.partial(fused_kernel, n, mine, momentum_decay, float(tokens * n) ** (-0.5)),
        out_shape=(
            jax.ShapeDtypeStruct((tokens, mine * width), bf16),
            jax.ShapeDtypeStruct(fast_weights.shape, f32),
        ),
        in_specs=[hbm, hbm, hbm, pl.BlockSpec(memory_space=pltpu.VMEM), hbm, hbm],
        out_specs=(hbm, hbm),
        scratch_shapes=[
            vmem((n, 3, mine, tokens, width), bf16),
            vmem((n, heads, 1, tokens), f32),
            vmem(fast_weights.shape, f32),
            vmem(fast_weights.shape, f32),
            vmem((mine, 3, 2 * rows, width), bf16),
            vmem((mine, 3, rows, width), bf16),
            vmem((mine, 3, rows, width), f32),
            vmem((mine, 3, rows, width), f32),
            vmem((mine, 3, 2 * rows, width), f32),
            vmem((mine, 3, 2 * rows, width), bf16),
            vmem((mine, 3, rows, width), bf16),
            vmem((mine, 3, rows, width), bf16),
            vmem((mine, tokens, width), f32),
            vmem((n, mine, tokens, width), bf16),
            vmem((n, mine, tokens, width), bf16),
            vmem((n, mine, tokens, width), bf16),
            vmem((tokens, mine * width), bf16),
            dma((4, max(mine, 2))),
            dma((2, n, 3, mine)),
            dma((n, 3, mine)),
            dma((2, n)),
            dma((n,)),
            dma((3,)),
            dma((3,)),
            dma((n, mine)),
            dma((2, n, mine)),
            dma((3,)),
        ],
        compiler_params=pltpu.CompilerParams(
            collective_id=0, has_side_effects=True, vmem_limit_bytes=56 * 1024 * 1024
        ),
    )(queries, key_vectors, values, learn_rates, fast_weights, momentum)


def per_device(*operands):
    queries, fast_weights = operands[0], operands[4]
    heads, _, rows, width = fast_weights.shape
    fits = lax.axis_size("rep") == 2 and heads % 2 == 0 and lax.axis_size("ctx") <= 4
    aligned = rows % 16 == 0 and width % 128 == 0 and queries.shape[0] == 128
    return (fused_device if fits and aligned else on_device)(*operands)


def solution(mesh):
    return jax.shard_map(
        per_device,
        mesh=mesh,
        in_specs=(
            P(("groups", "ctx"), "head"),
            P(("groups", "ctx"), "head"),
            P(("groups", "ctx"), "head"),
            P("head", ("groups", "ctx")),
            P(("groups", "head"), None, ("ctx", "rep"), None),
            P(("groups", "head"), None, ("ctx", "rep"), None),
        ),
        out_specs=(
            P(("groups", "ctx"), ("head", "rep")),
            P(("groups", "head"), None, ("ctx", "rep"), None),
        ),
        check_vma=False,
    )
```

```python
import functools

import jax
import jax.numpy as jnp
from jax import lax
from jax.experimental import pallas as pl
from jax.experimental.pallas import tpu as pltpu
from jax.sharding import PartitionSpec as P

epsilon = 1e-06
momentum_decay = 0.9


def passed_along(value, axis, steps):
    count = lax.axis_size(axis)
    initial, last = (max(0, -steps), min(count, count - steps))
    return lax.ppermute(value, axis, [(source, source + steps) for source in range(initial, last)])


def unit_rows(tensor):
    widened = tensor.astype(jnp.float32)
    factor = lax.rsqrt(jnp.mean(widened * widened, axis=-1, keepdims=True) + epsilon)
    return (widened * factor).astype(jnp.bfloat16)


def swiglu_apply(inputs, weights):
    gate = jnp.einsum("thd,hrd->htr", inputs, weights[:, 0], preferred_element_type=jnp.float32)
    upward = jnp.einsum("thd,hrd->htr", inputs, weights[:, 1], preferred_element_type=jnp.float32)
    hidden = (jax.nn.silu(gate) * upward).astype(jnp.bfloat16)
    return jnp.einsum("htr,hrd->htd", hidden, weights[:, 2], preferred_element_type=jnp.float32)


def window_attention(query_own, key_own, value_own, key_prior, value_prior, first_block):
    tok_rows = query_own.shape[0]
    per_rep = query_own.shape[1]
    width = query_own.shape[2]
    block_rows = min(tok_rows, 512)
    block_count = tok_rows // block_rows
    key_window = jnp.concatenate([key_prior, key_own], axis=0)
    value_window = jnp.concatenate([value_prior, value_own], axis=0)
    score_scale = width ** (-0.5)
    position = jnp.arange(2 * tok_rows)
    valid = jnp.logical_or(position >= tok_rows, jnp.logical_not(first_block))
    query_blocks = query_own.reshape(block_count, block_rows, per_rep, width)

    def one_block(query_block):
        scores = (
            jnp.einsum("tad,sad->ats", query_block, key_window, preferred_element_type=jnp.float32)
            * score_scale
        )
        scores = jnp.where(valid[None, None, :], scores, -jnp.inf)
        peak = jnp.max(scores, axis=-1, keepdims=True)
        weights = jnp.exp(scores - peak)
        probs = (weights / jnp.sum(weights, axis=-1, keepdims=True)).astype(jnp.bfloat16)
        return jnp.einsum("ats,sad->tad", probs, value_window, preferred_element_type=jnp.float32)

    return lax.map(one_block, query_blocks).reshape(tok_rows, per_rep, width)


def on_device(queries, key_vectors, values, learn_rates, fast_weights, momentum):
    tok_rows = queries.shape[0]
    head_count = fast_weights.shape[0]
    width = fast_weights.shape[3]
    rep_count = lax.axis_size("rep")
    per_rep = head_count // rep_count
    rep_index = lax.axis_index("rep")
    ctx_index = lax.axis_index("ctx")
    total_tokens = tok_rows * lax.axis_size("ctx")
    query_heads = queries.reshape(tok_rows, head_count, width)
    key_heads = key_vectors.reshape(tok_rows, head_count, width)
    value_heads = values.reshape(tok_rows, head_count, width)
    query_unit = unit_rows(query_heads)
    key_unit = unit_rows(key_heads)
    token_scale = float(total_tokens) ** (-0.5)
    cotangent = (
        -(learn_rates.T[:, :, None] * token_scale) * value_heads.astype(jnp.float32)
    ).astype(jnp.bfloat16)
    weight_rows = lax.all_gather(fast_weights.astype(jnp.bfloat16), "ctx", axis=2, tiled=True)
    gate = jnp.einsum(
        "thd,hrd->htr", key_unit, weight_rows[:, 0], preferred_element_type=jnp.float32
    )
    upward = jnp.einsum(
        "thd,hrd->htr", key_unit, weight_rows[:, 1], preferred_element_type=jnp.float32
    )
    back = jnp.einsum(
        "thd,hrd->htr", cotangent, weight_rows[:, 2], preferred_element_type=jnp.float32
    )
    sigma = jax.nn.sigmoid(gate)
    activated = jax.nn.silu(gate)
    hidden = (activated * upward).astype(jnp.bfloat16)
    gate_back = (back * upward * sigma * (1.0 + gate * (1.0 - sigma))).astype(jnp.bfloat16)
    up_back = (back * activated).astype(jnp.bfloat16)
    grad_gate = jnp.einsum("htr,thd->hrd", gate_back, key_unit, preferred_element_type=jnp.float32)
    grad_up = jnp.einsum("htr,thd->hrd", up_back, key_unit, preferred_element_type=jnp.float32)
    grad_down = jnp.einsum("htr,thd->hrd", hidden, cotangent, preferred_element_type=jnp.float32)
    gradient = jnp.stack([grad_gate, grad_up, grad_down], axis=1)
    share = lax.psum_scatter(
        gradient.astype(jnp.bfloat16), "ctx", scatter_dimension=2, tiled=True
    ).astype(jnp.float32)
    fast_updated = fast_weights - (momentum_decay * momentum + share)
    new_rows = lax.all_gather(fast_updated.astype(jnp.bfloat16), "ctx", axis=2, tiled=True)
    own_start = rep_index * per_rep
    partial_out = swiglu_apply(query_unit, new_rows)
    traded = lax.all_to_all(
        partial_out.astype(jnp.bfloat16), "rep", split_axis=0, concat_axis=0, tiled=True
    ).astype(partial_out.dtype)
    fast_out = jnp.sum(traded.reshape(rep_count, per_rep, tok_rows, width), axis=0)
    attend_query = lax.dynamic_slice_in_dim(query_heads, own_start, per_rep, 1)
    attend_key = lax.dynamic_slice_in_dim(key_heads, own_start, per_rep, 1)
    attend_value = lax.dynamic_slice_in_dim(value_heads, own_start, per_rep, 1)
    key_prior, value_prior = passed_along((attend_key, attend_value), "ctx", 1)
    attended = window_attention(
        attend_query, attend_key, attend_value, key_prior, value_prior, ctx_index == 0
    )
    combined = attended + jnp.transpose(fast_out, (1, 0, 2))
    layer_output = combined.astype(jnp.bfloat16).reshape(tok_rows, per_rep * width)
    return (layer_output, fast_updated)


def contract(left, right, left_dim, right_dim):
    return lax.dot_general(
        left, right, (((left_dim,), (right_dim,)), ((), ())), preferred_element_type=jnp.float32
    )


def fused_kernel(
    n, mine, decay, token_scale,
    q_hbm, k_hbm, v_hbm, lr_ref, fw_hbm, mom_hbm,
    out_hbm, fast_hbm,
    tok, lrs, fw, mom, weights, w_send, base_peer, base_send, grad, new_w, g_send, g_recv,
    attn, part, sums_right, sums_left, out_v,
    in_sem, tok_send, tok_recv, lr_send, lr_recv, pair_send, pair_recv, sum_send, sum_recv, out_sem,
):
    MESH = pl.DeviceIdType.MESH
    z = lax.axis_index("ctx")
    r = lax.axis_index("rep")
    heads, _, rows, width = fw.shape
    piece = part.shape[2]
    cuts = tok.shape[3] // piece
    has_left, has_right = z > 0, z < n - 1
    own, other = r * mine, (1 - r) * mine

    def load(c, h):
        ref = (k_hbm, v_hbm, q_hbm)[c]
        column = pl.multiple_of((own + h) * width, 128)
        return pltpu.make_async_copy(ref.at[:, pl.ds(column, width)], tok.at[z, c, h], in_sem.at[c, h])

    for c in range(3):
        for h in range(mine):
            load(c, h).start()
    load_fw = pltpu.make_async_copy(fw_hbm, fw, in_sem.at[3, 0])
    load_mom = pltpu.make_async_copy(mom_hbm, mom, in_sem.at[3, 1])
    load_fw.start()
    load_mom.start()
    for i in range(heads):
        lrs[z, i] = lr_ref[i : i + 1, :] * (-token_scale)

    barrier = pltpu.get_barrier_semaphore()
    pl.semaphore_signal(barrier, inc=1, device_id={"rep": 1 - r}, device_id_type=MESH)

    @pl.when(has_left)
    def _():
        pl.semaphore_signal(barrier, inc=1, device_id={"ctx": z - 1}, device_id_type=MESH)

    @pl.when(has_right)
    def _():
        pl.semaphore_signal(barrier, inc=1, device_id={"ctx": z + 1}, device_id_type=MESH)

    pl.semaphore_wait(barrier, 1 + has_left.astype(jnp.int32) + has_right.astype(jnp.int32))

    def tok_copy(b, c, h, way):
        return pltpu.make_async_remote_copy(
            src_ref=tok.at[b, c, h], dst_ref=tok.at[b, c, h],
            send_sem=tok_send.at[way, b, c, h], recv_sem=tok_recv.at[b, c, h],
            device_id={"ctx": z + 1 - 2 * way}, device_id_type=MESH,
        )

    def lr_copy(b, way):
        return pltpu.make_async_remote_copy(
            src_ref=lrs.at[b], dst_ref=lrs.at[b],
            send_sem=lr_send.at[way, b], recv_sem=lr_recv.at[b],
            device_id={"ctx": z + 1 - 2 * way}, device_id_type=MESH,
        )

    def pair_copy(which):
        src, dst = (
            (w_send, weights.at[:, :, pl.ds(rows, rows), :]),
            (base_send, base_peer),
            (g_send, g_recv),
        )[which]
        return pltpu.make_async_remote_copy(
            src_ref=src, dst_ref=dst, send_sem=pair_send.at[which], recv_sem=pair_recv.at[which],
            device_id={"rep": 1 - r}, device_id_type=MESH,
        )

    def sum_copy(b, h, way):
        return pltpu.make_async_remote_copy(
            src_ref=part.at[b, h], dst_ref=(sums_right, sums_left)[way].at[b, h],
            send_sem=sum_send.at[b, h], recv_sem=sum_recv.at[way, b, h],
            device_id={"ctx": z + 1 - 2 * way}, device_id_type=MESH,
        )

    open_way = (has_right, has_left)

    def own_send(make):
        for way in range(2):
            pl.when(open_way[way])(lambda way=way: make(way).start())

    own_send(lambda way: lr_copy(z, way))
    for h in range(mine):
        for c in range(2):
            load(c, h).wait()
            own_send(lambda way: tok_copy(z, c, h, way))
    for h in range(mine):
        load(2, h).wait()

    def own_queries(step):
        for way in range(2):
            last = z if way == 0 else n - 1 - z

            @pl.when(jnp.logical_and(step == last, open_way[way]))
            def _(way=way):
                for h in range(mine):
                    tok_copy(z, 2, h, way).start()

    own_queries(0)

    load_fw.wait()
    for h in range(mine):
        for m in range(3):
            w_send[h, m] = fw[other + h, m].astype(jnp.bfloat16)
    pair_copy(0).start()
    for h in range(mine):
        for m in range(3):
            weights[h, m, :rows] = fw[own + h, m].astype(jnp.bfloat16)
    load_mom.wait()
    for h in range(mine):
        for m in range(3):
            base_send[h, m] = fw[other + h, m] - decay * mom[other + h, m]
    pair_copy(1).start()
    pair_copy(0).wait_recv()

    def grad_block(b, first):
        @pl.loop(0, mine)
        def _(h):
            key = unit_rows(tok[b, 0, h])
            value = tok[b, 1, h]
            rate = lrs[b, own + h]
            both = contract(weights[h, 0:2].reshape(4 * rows, width), key, 1, 1)
            gate, upward = both[: 2 * rows], both[2 * rows :]
            back = contract(weights[h, 2], value, 1, 1) * rate
            sigma = jax.nn.sigmoid(gate)
            activated = gate * sigma
            hidden = (activated * upward * rate).astype(jnp.bfloat16)
            gate_back = (back * upward * sigma * (1.0 + gate * (1.0 - sigma))).astype(jnp.bfloat16)
            up_back = (back * activated).astype(jnp.bfloat16)
            terms = (
                contract(gate_back, key, 1, 0),
                contract(up_back, key, 1, 0),
                contract(hidden, value, 1, 0),
            )
            for m in range(3):
                grad[h, m] = terms[m] if first else grad[h, m] + terms[m]

    def attend(with_prior):
        @pl.loop(0, mine)
        def _(h):
            query = tok[z, 2, h]
            scale = width ** (-0.5)
            scores = contract(query, tok[z, 0, h], 1, 1) * scale
            peak = jnp.max(scores, axis=-1, keepdims=True)
            if with_prior:
                prior = contract(query, tok[z - 1, 0, h], 1, 1) * scale
                peak = jnp.maximum(peak, jnp.max(prior, axis=-1, keepdims=True))
                prior = jnp.exp(prior - peak)
            scores = jnp.exp(scores - peak)
            total = jnp.sum(scores, axis=-1, keepdims=True)
            if with_prior:
                total = total + jnp.sum(prior, axis=-1, keepdims=True)
            result = contract((scores / total).astype(jnp.bfloat16), tok[z, 1, h], 1, 0)
            if with_prior:
                result = result + contract((prior / total).astype(jnp.bfloat16), tok[z - 1, 1, h], 1, 0)
            attn[h] = result

    def from_left(step):
        return z - step >= 0

    def from_right(step):
        return z + step < n

    grad_block(z, True)

    @pl.when(z == 0)
    def _():
        attend(False)

    def pass_on(step, pieces, with_lr):
        arrives = (from_left(step), from_right(step))
        for way in range(2):
            b = z - step if way == 0 else z + step
            if with_lr:
                @pl.when(arrives[way])
                def _(way=way, b=b):
                    lr_copy(b, way).wait_recv()
                    pl.when(open_way[way])(lambda: lr_copy(b, way).start())

        for c, h in pieces:
            for way in range(2):
                b = z - step if way == 0 else z + step

                @pl.when(arrives[way])
                def _(way=way, b=b):
                    tok_copy(b, c, h, way).wait_recv()
                    pl.when(open_way[way])(lambda: tok_copy(b, c, h, way).start())

    def keys_step(step, carry):
        pass_on(step, [(c, h) for h in range(mine) for c in range(2)], True)
        own_queries(step)

        @pl.when(from_left(step))
        def _():
            grad_block(z - step, False)

        @pl.when(from_right(step))
        def _():
            grad_block(z + step, False)

        @pl.when(jnp.logical_and(step == 1, has_left))
        def _():
            attend(True)

        return carry

    lax.fori_loop(1, n, keys_step, 0)

    pair_copy(1).wait_recv()
    for h in range(mine):
        for m in range(3):
            fresh = fw[own + h, m] - (decay * mom[own + h, m] + grad[h, m, :rows])
            fw[own + h, m] = fresh
            new_w[h, m, :rows] = fresh.astype(jnp.bfloat16)
            new_w[h, m, rows:] = (base_peer[h, m] - grad[h, m, rows:]).astype(jnp.bfloat16)
            g_send[h, m] = grad[h, m, rows:].astype(jnp.bfloat16)
    pair_copy(2).start()
    store_own = pltpu.make_async_copy(
        fw.at[pl.ds(own, mine)], fast_hbm.at[pl.ds(own, mine)], out_sem.at[0]
    )
    store_own.start()

    def apply(b, h):
        query = unit_rows(tok[b, 2, h])
        gate = contract(query, new_w[h, 0], 1, 1)
        upward = contract(query, new_w[h, 1], 1, 1)
        hidden = (gate * jax.nn.sigmoid(gate) * upward).astype(jnp.bfloat16)
        return contract(hidden, new_w[h, 2], 1, 0)

    @pl.loop(0, mine)
    def _(h):
        attn[h] = attn[h] + apply(z, h)

    def queries_step(step, carry):
        for h in range(mine):
            pass_on(step, [(2, h)], False)
            for way in range(2):
                b = z - step if way == 1 else z + step
                source_there = from_left(step) if way == 1 else from_right(step)
                starts_here = jnp.logical_not(has_right if way == 1 else has_left)

                @pl.when(source_there)
                def _(b=b, way=way, starts_here=starts_here):
                    result = apply(b, h).astype(jnp.bfloat16)
                    for half in range(cuts):
                        part[b, cuts * h + half] = result[half * piece : (half + 1) * piece]

                    @pl.when(starts_here)
                    def _():
                        for half in range(cuts):
                            sum_copy(b, cuts * h + half, way).start()

        return carry

    lax.fori_loop(1, n, queries_step, 0)

    near_left = 2 * z < n - 1

    def merge_step(step, carry):
        for h in range(cuts * mine):
            for way, turn in ((0, near_left), (1, None), (0, jnp.logical_not(near_left))):
                b = step if way == 0 else n - 1 - step
                there = jnp.logical_and(b > z, has_left) if way == 0 else jnp.logical_and(b < z, has_right)

                @pl.when(there if turn is None else jnp.logical_and(there, turn))
                def _(b=b, way=way):
                    sum_copy(b, h, way).wait_recv()
                    arrived = (sums_right, sums_left)[way][b, h].astype(jnp.float32)
                    part[b, h] = (part[b, h].astype(jnp.float32) + arrived).astype(jnp.bfloat16)
                    sum_copy(b, h, way).start()

        return carry

    lax.fori_loop(1, n, merge_step, 0)

    pair_copy(2).wait_recv()
    for h in range(mine):
        for m in range(3):
            fw[other + h, m] = fw[other + h, m] - (
                decay * mom[other + h, m] + g_recv[h, m].astype(jnp.float32)
            )
    store_other = pltpu.make_async_copy(
        fw.at[pl.ds(other, mine)], fast_hbm.at[pl.ds(other, mine)], out_sem.at[1]
    )
    store_other.start()

    for p in range(cuts * mine):
        h, at = p // cuts, pl.ds(p % cuts * piece, piece)

        @pl.when(has_left)
        def _():
            sum_copy(z, p, 0).wait_recv()
            attn[h, at] = attn[h, at] + sums_right[z, p].astype(jnp.float32)

        @pl.when(has_right)
        def _():
            sum_copy(z, p, 1).wait_recv()
            attn[h, at] = attn[h, at] + sums_left[z, p].astype(jnp.float32)

        out_v[at, h * width : (h + 1) * width] = attn[h, at].astype(jnp.bfloat16)
    store_out = pltpu.make_async_copy(out_v, out_hbm, out_sem.at[2])
    store_out.start()

    for way in range(2):
        @pl.when(open_way[way])
        def _(way=way):
            lr_copy(z, way).wait_send()
            for h in range(mine):
                for c in range(3):
                    tok_copy(z, c, h, way).wait_send()

    def drain(step, carry):
        for way in range(2):
            b = z - step if way == 0 else z + step
            arrives = from_left(step) if way == 0 else from_right(step)

            @pl.when(jnp.logical_and(arrives, open_way[way]))
            def _(way=way, b=b):
                lr_copy(b, way).wait_send()
                for h in range(mine):
                    for c in range(3):
                        tok_copy(b, c, h, way).wait_send()

            @pl.when(arrives)
            def _(way=way, b=b):
                for p in range(cuts * mine):
                    sum_copy(b, p, 1 - way).wait_send()

        return carry

    lax.fori_loop(1, n, drain, 0)
    for which in range(3):
        pair_copy(which).wait_send()
    store_own.wait()
    store_other.wait()
    store_out.wait()


def fused_device(queries, key_vectors, values, learn_rates, fast_weights, momentum):
    n = lax.axis_size("ctx")
    tokens = queries.shape[0]
    heads, _, rows, width = fast_weights.shape
    mine = heads // 2
    cuts = 2
    bf16, f32 = jnp.bfloat16, jnp.float32
    hbm = pl.BlockSpec(memory_space=pl.ANY)
    dma = pltpu.SemaphoreType.DMA
    vmem = pltpu.VMEM
    return pl.pallas_call(
        functools.partial(fused_kernel, n, mine, momentum_decay, float(tokens * n) ** (-0.5)),
        out_shape=(
            jax.ShapeDtypeStruct((tokens, mine * width), bf16),
            jax.ShapeDtypeStruct(fast_weights.shape, f32),
        ),
        in_specs=[hbm, hbm, hbm, pl.BlockSpec(memory_space=pltpu.VMEM), hbm, hbm],
        out_specs=(hbm, hbm),
        scratch_shapes=[
            vmem((n, 3, mine, tokens, width), bf16),
            vmem((n, heads, 1, tokens), f32),
            vmem(fast_weights.shape, f32),
            vmem(fast_weights.shape, f32),
            vmem((mine, 3, 2 * rows, width), bf16),
            vmem((mine, 3, rows, width), bf16),
            vmem((mine, 3, rows, width), f32),
            vmem((mine, 3, rows, width), f32),
            vmem((mine, 3, 2 * rows, width), f32),
            vmem((mine, 3, 2 * rows, width), bf16),
            vmem((mine, 3, rows, width), bf16),
            vmem((mine, 3, rows, width), bf16),
            vmem((mine, tokens, width), f32),
            vmem((n, cuts * mine, tokens // cuts, width), bf16),
            vmem((n, cuts * mine, tokens // cuts, width), bf16),
            vmem((n, cuts * mine, tokens // cuts, width), bf16),
            vmem((tokens, mine * width), bf16),
            dma((4, max(mine, 2))),
            dma((2, n, 3, mine)),
            dma((n, 3, mine)),
            dma((2, n)),
            dma((n,)),
            dma((3,)),
            dma((3,)),
            dma((n, cuts * mine)),
            dma((2, n, cuts * mine)),
            dma((3,)),
        ],
        compiler_params=pltpu.CompilerParams(
            collective_id=0, has_side_effects=True, vmem_limit_bytes=56 * 1024 * 1024
        ),
    )(queries, key_vectors, values, learn_rates, fast_weights, momentum)


def per_device(*operands):
    queries, fast_weights = operands[0], operands[4]
    heads, _, rows, width = fast_weights.shape
    fits = lax.axis_size("rep") == 2 and heads % 2 == 0 and lax.axis_size("ctx") <= 4
    aligned = rows % 16 == 0 and width % 128 == 0 and queries.shape[0] == 128
    return (fused_device if fits and aligned else on_device)(*operands)


def solution(mesh):
    return jax.shard_map(
        per_device,
        mesh=mesh,
        in_specs=(
            P(("groups", "ctx"), "head"),
            P(("groups", "ctx"), "head"),
            P(("groups", "ctx"), "head"),
            P("head", ("groups", "ctx")),
            P(("groups", "head"), None, ("ctx", "rep"), None),
            P(("groups", "head"), None, ("ctx", "rep"), None),
        ),
        out_specs=(
            P(("groups", "ctx"), ("head", "rep")),
            P(("groups", "head"), None, ("ctx", "rep"), None),
        ),
        check_vma=False,
    )
```

```python
import functools

import jax
import jax.numpy as jnp
from jax import lax
from jax.experimental import pallas as pl
from jax.experimental.pallas import tpu as pltpu
from jax.sharding import PartitionSpec as P

epsilon = 1e-06
momentum_decay = 0.9


def passed_along(value, axis, steps):
    count = lax.axis_size(axis)
    initial, last = (max(0, -steps), min(count, count - steps))
    return lax.ppermute(value, axis, [(source, source + steps) for source in range(initial, last)])


def unit_rows(tensor):
    widened = tensor.astype(jnp.float32)
    factor = lax.rsqrt(jnp.mean(widened * widened, axis=-1, keepdims=True) + epsilon)
    return (widened * factor).astype(jnp.bfloat16)


def swiglu_apply(inputs, weights):
    gate = jnp.einsum("thd,hrd->htr", inputs, weights[:, 0], preferred_element_type=jnp.float32)
    upward = jnp.einsum("thd,hrd->htr", inputs, weights[:, 1], preferred_element_type=jnp.float32)
    hidden = (jax.nn.silu(gate) * upward).astype(jnp.bfloat16)
    return jnp.einsum("htr,hrd->htd", hidden, weights[:, 2], preferred_element_type=jnp.float32)


def window_attention(query_own, key_own, value_own, key_prior, value_prior, first_block):
    tok_rows = query_own.shape[0]
    per_rep = query_own.shape[1]
    width = query_own.shape[2]
    block_rows = min(tok_rows, 512)
    block_count = tok_rows // block_rows
    key_window = jnp.concatenate([key_prior, key_own], axis=0)
    value_window = jnp.concatenate([value_prior, value_own], axis=0)
    score_scale = width ** (-0.5)
    position = jnp.arange(2 * tok_rows)
    valid = jnp.logical_or(position >= tok_rows, jnp.logical_not(first_block))
    query_blocks = query_own.reshape(block_count, block_rows, per_rep, width)

    def one_block(query_block):
        scores = (
            jnp.einsum("tad,sad->ats", query_block, key_window, preferred_element_type=jnp.float32)
            * score_scale
        )
        scores = jnp.where(valid[None, None, :], scores, -jnp.inf)
        peak = jnp.max(scores, axis=-1, keepdims=True)
        weights = jnp.exp(scores - peak)
        probs = (weights / jnp.sum(weights, axis=-1, keepdims=True)).astype(jnp.bfloat16)
        return jnp.einsum("ats,sad->tad", probs, value_window, preferred_element_type=jnp.float32)

    return lax.map(one_block, query_blocks).reshape(tok_rows, per_rep, width)


def on_device(queries, key_vectors, values, learn_rates, fast_weights, momentum):
    tok_rows = queries.shape[0]
    head_count = fast_weights.shape[0]
    width = fast_weights.shape[3]
    rep_count = lax.axis_size("rep")
    per_rep = head_count // rep_count
    rep_index = lax.axis_index("rep")
    ctx_index = lax.axis_index("ctx")
    total_tokens = tok_rows * lax.axis_size("ctx")
    query_heads = queries.reshape(tok_rows, head_count, width)
    key_heads = key_vectors.reshape(tok_rows, head_count, width)
    value_heads = values.reshape(tok_rows, head_count, width)
    query_unit = unit_rows(query_heads)
    key_unit = unit_rows(key_heads)
    token_scale = float(total_tokens) ** (-0.5)
    cotangent = (
        -(learn_rates.T[:, :, None] * token_scale) * value_heads.astype(jnp.float32)
    ).astype(jnp.bfloat16)
    weight_rows = lax.all_gather(fast_weights.astype(jnp.bfloat16), "ctx", axis=2, tiled=True)
    gate = jnp.einsum(
        "thd,hrd->htr", key_unit, weight_rows[:, 0], preferred_element_type=jnp.float32
    )
    upward = jnp.einsum(
        "thd,hrd->htr", key_unit, weight_rows[:, 1], preferred_element_type=jnp.float32
    )
    back = jnp.einsum(
        "thd,hrd->htr", cotangent, weight_rows[:, 2], preferred_element_type=jnp.float32
    )
    sigma = jax.nn.sigmoid(gate)
    activated = jax.nn.silu(gate)
    hidden = (activated * upward).astype(jnp.bfloat16)
    gate_back = (back * upward * sigma * (1.0 + gate * (1.0 - sigma))).astype(jnp.bfloat16)
    up_back = (back * activated).astype(jnp.bfloat16)
    grad_gate = jnp.einsum("htr,thd->hrd", gate_back, key_unit, preferred_element_type=jnp.float32)
    grad_up = jnp.einsum("htr,thd->hrd", up_back, key_unit, preferred_element_type=jnp.float32)
    grad_down = jnp.einsum("htr,thd->hrd", hidden, cotangent, preferred_element_type=jnp.float32)
    gradient = jnp.stack([grad_gate, grad_up, grad_down], axis=1)
    share = lax.psum_scatter(
        gradient.astype(jnp.bfloat16), "ctx", scatter_dimension=2, tiled=True
    ).astype(jnp.float32)
    fast_updated = fast_weights - (momentum_decay * momentum + share)
    new_rows = lax.all_gather(fast_updated.astype(jnp.bfloat16), "ctx", axis=2, tiled=True)
    own_start = rep_index * per_rep
    partial_out = swiglu_apply(query_unit, new_rows)
    traded = lax.all_to_all(
        partial_out.astype(jnp.bfloat16), "rep", split_axis=0, concat_axis=0, tiled=True
    ).astype(partial_out.dtype)
    fast_out = jnp.sum(traded.reshape(rep_count, per_rep, tok_rows, width), axis=0)
    attend_query = lax.dynamic_slice_in_dim(query_heads, own_start, per_rep, 1)
    attend_key = lax.dynamic_slice_in_dim(key_heads, own_start, per_rep, 1)
    attend_value = lax.dynamic_slice_in_dim(value_heads, own_start, per_rep, 1)
    key_prior, value_prior = passed_along((attend_key, attend_value), "ctx", 1)
    attended = window_attention(
        attend_query, attend_key, attend_value, key_prior, value_prior, ctx_index == 0
    )
    combined = attended + jnp.transpose(fast_out, (1, 0, 2))
    layer_output = combined.astype(jnp.bfloat16).reshape(tok_rows, per_rep * width)
    return (layer_output, fast_updated)


def contract(left, right, left_dim, right_dim):
    return lax.dot_general(
        left, right, (((left_dim,), (right_dim,)), ((), ())), preferred_element_type=jnp.float32
    )


def fused_kernel(
    n, mine, decay, token_scale,
    q_hbm, k_hbm, v_hbm, lr_ref, fw_hbm, mom_hbm,
    out_hbm, fast_hbm,
    tok, lrs, fw, mom, weights, w_send, base_peer, base_send, grad, new_w, g_send, g_recv,
    attn, part, sums_right, sums_left, out_v,
    in_sem, tok_send, tok_recv, lr_send, lr_recv, pair_send, pair_recv, sum_send, sum_recv, out_sem,
):
    MESH = pl.DeviceIdType.MESH
    z = lax.axis_index("ctx")
    r = lax.axis_index("rep")
    heads, _, rows, width = fw.shape
    piece = part.shape[2]
    cuts = tok.shape[3] // piece
    has_left, has_right = z > 0, z < n - 1
    own, other = r * mine, (1 - r) * mine

    def load(c, h):
        ref = (k_hbm, v_hbm, q_hbm)[c]
        column = pl.multiple_of((own + h) * width, 128)
        return pltpu.make_async_copy(ref.at[:, pl.ds(column, width)], tok.at[z, c, h], in_sem.at[c, h])

    for c in range(3):
        for h in range(mine):
            load(c, h).start()
    load_fw = pltpu.make_async_copy(fw_hbm, fw, in_sem.at[3, 0])
    load_mom = pltpu.make_async_copy(mom_hbm, mom, in_sem.at[3, 1])
    load_fw.start()
    load_mom.start()
    for i in range(heads):
        lrs[z, i] = lr_ref[i : i + 1, :] * (-token_scale)

    barrier = pltpu.get_barrier_semaphore()
    pl.semaphore_signal(barrier, inc=1, device_id={"rep": 1 - r}, device_id_type=MESH)

    @pl.when(has_left)
    def _():
        pl.semaphore_signal(barrier, inc=1, device_id={"ctx": z - 1}, device_id_type=MESH)

    @pl.when(has_right)
    def _():
        pl.semaphore_signal(barrier, inc=1, device_id={"ctx": z + 1}, device_id_type=MESH)

    pl.semaphore_wait(barrier, 1 + has_left.astype(jnp.int32) + has_right.astype(jnp.int32))

    def tok_copy(b, c, h, way):
        return pltpu.make_async_remote_copy(
            src_ref=tok.at[b, c, h], dst_ref=tok.at[b, c, h],
            send_sem=tok_send.at[way, b, c, h], recv_sem=tok_recv.at[b, c, h],
            device_id={"ctx": z + 1 - 2 * way}, device_id_type=MESH,
        )

    def lr_copy(b, way):
        return pltpu.make_async_remote_copy(
            src_ref=lrs.at[b], dst_ref=lrs.at[b],
            send_sem=lr_send.at[way, b], recv_sem=lr_recv.at[b],
            device_id={"ctx": z + 1 - 2 * way}, device_id_type=MESH,
        )

    def pair_copy(which):
        src, dst = (
            (w_send, weights.at[:, :, pl.ds(rows, rows), :]),
            (base_send, base_peer),
            (g_send, g_recv),
        )[which]
        return pltpu.make_async_remote_copy(
            src_ref=src, dst_ref=dst, send_sem=pair_send.at[which], recv_sem=pair_recv.at[which],
            device_id={"rep": 1 - r}, device_id_type=MESH,
        )

    def sum_copy(b, h, way):
        return pltpu.make_async_remote_copy(
            src_ref=part.at[b, h], dst_ref=(sums_right, sums_left)[way].at[b, h],
            send_sem=sum_send.at[b, h], recv_sem=sum_recv.at[way, b, h],
            device_id={"ctx": z + 1 - 2 * way}, device_id_type=MESH,
        )

    open_way = (has_right, has_left)

    def own_send(make):
        for way in range(2):
            pl.when(open_way[way])(lambda way=way: make(way).start())

    own_send(lambda way: lr_copy(z, way))
    for h in range(mine):
        for c in range(2):
            load(c, h).wait()
            own_send(lambda way: tok_copy(z, c, h, way))
    for h in range(mine):
        load(2, h).wait()

    def own_queries(step):
        for way in range(2):
            last = z if way == 0 else n - 1 - z

            @pl.when(jnp.logical_and(step == last, open_way[way]))
            def _(way=way):
                for h in range(mine):
                    tok_copy(z, 2, h, way).start()

    own_queries(0)

    load_fw.wait()
    for h in range(mine):
        for m in range(3):
            w_send[h, m] = fw[other + h, m].astype(jnp.bfloat16)
    pair_copy(0).start()
    for h in range(mine):
        for m in range(3):
            weights[h, m, :rows] = fw[own + h, m].astype(jnp.bfloat16)
    load_mom.wait()
    for h in range(mine):
        for m in range(3):
            base_send[h, m] = fw[other + h, m] - decay * mom[other + h, m]
    pair_copy(1).start()
    pair_copy(0).wait_recv()

    def grad_block(b, first):
        @pl.loop(0, mine)
        def _(h):
            key = unit_rows(tok[b, 0, h])
            value = tok[b, 1, h]
            rate = lrs[b, own + h]
            both = contract(weights[h, 0:2].reshape(4 * rows, width), key, 1, 1)
            gate, upward = both[: 2 * rows], both[2 * rows :]
            back = contract(weights[h, 2], value, 1, 1) * rate
            sigma = jax.nn.sigmoid(gate)
            activated = gate * sigma
            hidden = (activated * upward * rate).astype(jnp.bfloat16)
            gate_back = (back * upward * sigma * (1.0 + gate * (1.0 - sigma))).astype(jnp.bfloat16)
            up_back = (back * activated).astype(jnp.bfloat16)
            terms = (
                contract(gate_back, key, 1, 0),
                contract(up_back, key, 1, 0),
                contract(hidden, value, 1, 0),
            )
            for m in range(3):
                grad[h, m] = terms[m] if first else grad[h, m] + terms[m]

    def attend(with_prior):
        @pl.loop(0, mine)
        def _(h):
            query = tok[z, 2, h]
            scale = width ** (-0.5)
            scores = contract(query, tok[z, 0, h], 1, 1) * scale
            peak = jnp.max(scores, axis=-1, keepdims=True)
            if with_prior:
                prior = contract(query, tok[z - 1, 0, h], 1, 1) * scale
                peak = jnp.maximum(peak, jnp.max(prior, axis=-1, keepdims=True))
                prior = jnp.exp(prior - peak)
            scores = jnp.exp(scores - peak)
            total = jnp.sum(scores, axis=-1, keepdims=True)
            if with_prior:
                total = total + jnp.sum(prior, axis=-1, keepdims=True)
            result = contract((scores / total).astype(jnp.bfloat16), tok[z, 1, h], 1, 0)
            if with_prior:
                result = result + contract((prior / total).astype(jnp.bfloat16), tok[z - 1, 1, h], 1, 0)
            attn[h] = result

    def from_left(step):
        return z - step >= 0

    def from_right(step):
        return z + step < n

    grad_block(z, True)

    @pl.when(z == 0)
    def _():
        attend(False)

    def pass_on(step, pieces, with_lr):
        arrives = (from_left(step), from_right(step))
        for way in range(2):
            b = z - step if way == 0 else z + step
            if with_lr:
                @pl.when(arrives[way])
                def _(way=way, b=b):
                    lr_copy(b, way).wait_recv()
                    pl.when(open_way[way])(lambda: lr_copy(b, way).start())

        for c, h in pieces:
            for way in range(2):
                b = z - step if way == 0 else z + step

                @pl.when(arrives[way])
                def _(way=way, b=b):
                    tok_copy(b, c, h, way).wait_recv()
                    pl.when(open_way[way])(lambda: tok_copy(b, c, h, way).start())

    def keys_step(step, carry):
        pass_on(step, [(c, h) for h in range(mine) for c in range(2)], True)
        own_queries(step)

        @pl.when(from_left(step))
        def _():
            grad_block(z - step, False)

        @pl.when(from_right(step))
        def _():
            grad_block(z + step, False)

        @pl.when(jnp.logical_and(step == 1, has_left))
        def _():
            attend(True)

        return carry

    lax.fori_loop(1, n, keys_step, 0)

    pair_copy(1).wait_recv()
    for h in range(mine):
        for m in range(3):
            fresh = fw[own + h, m] - (decay * mom[own + h, m] + grad[h, m, :rows])
            fw[own + h, m] = fresh
            new_w[h, m, :rows] = fresh.astype(jnp.bfloat16)
            new_w[h, m, rows:] = (base_peer[h, m] - grad[h, m, rows:]).astype(jnp.bfloat16)
            g_send[h, m] = grad[h, m, rows:].astype(jnp.bfloat16)
    pair_copy(2).start()
    store_own = pltpu.make_async_copy(
        fw.at[pl.ds(own, mine)], fast_hbm.at[pl.ds(own, mine)], out_sem.at[0]
    )
    store_own.start()

    def apply(b, h):
        query = unit_rows(tok[b, 2, h])
        gate = contract(query, new_w[h, 0], 1, 1)
        upward = contract(query, new_w[h, 1], 1, 1)
        hidden = (gate * jax.nn.sigmoid(gate) * upward).astype(jnp.bfloat16)
        return contract(hidden, new_w[h, 2], 1, 0)

    @pl.loop(0, mine)
    def _(h):
        attn[h] = attn[h] + apply(z, h)

    def queries_step(step, carry):
        for h in range(mine):
            pass_on(step, [(2, h)], False)
            for way in range(2):
                b = z - step if way == 1 else z + step
                source_there = from_left(step) if way == 1 else from_right(step)
                starts_here = jnp.logical_not(has_right if way == 1 else has_left)

                @pl.when(source_there)
                def _(b=b, way=way, starts_here=starts_here):
                    result = apply(b, h).astype(jnp.bfloat16)
                    for half in range(cuts):
                        part[b, cuts * h + half] = result[half * piece : (half + 1) * piece]

                    @pl.when(starts_here)
                    def _():
                        for half in range(cuts):
                            sum_copy(b, cuts * h + half, way).start()

        return carry

    lax.fori_loop(1, n, queries_step, 0)

    near_left = 2 * z < n - 1

    def merge_step(step, carry):
        for h in range(cuts * mine):
            for way, turn in ((0, near_left), (1, None), (0, jnp.logical_not(near_left))):
                b = step if way == 0 else n - 1 - step
                there = jnp.logical_and(b > z, has_left) if way == 0 else jnp.logical_and(b < z, has_right)

                @pl.when(there if turn is None else jnp.logical_and(there, turn))
                def _(b=b, way=way):
                    sum_copy(b, h, way).wait_recv()
                    arrived = (sums_right, sums_left)[way][b, h].astype(jnp.float32)
                    part[b, h] = (part[b, h].astype(jnp.float32) + arrived).astype(jnp.bfloat16)
                    sum_copy(b, h, way).start()

        return carry

    lax.fori_loop(1, n, merge_step, 0)

    pair_copy(2).wait_recv()
    for h in range(mine):
        for m in range(3):
            fw[other + h, m] = fw[other + h, m] - (
                decay * mom[other + h, m] + g_recv[h, m].astype(jnp.float32)
            )
    store_other = pltpu.make_async_copy(
        fw.at[pl.ds(other, mine)], fast_hbm.at[pl.ds(other, mine)], out_sem.at[1]
    )
    store_other.start()

    for p in range(cuts * mine):
        h, at = p // cuts, pl.ds(p % cuts * piece, piece)

        @pl.when(has_left)
        def _():
            sum_copy(z, p, 0).wait_recv()
            attn[h, at] = attn[h, at] + sums_right[z, p].astype(jnp.float32)

        @pl.when(has_right)
        def _():
            sum_copy(z, p, 1).wait_recv()
            attn[h, at] = attn[h, at] + sums_left[z, p].astype(jnp.float32)

        out_v[at, h * width : (h + 1) * width] = attn[h, at].astype(jnp.bfloat16)
    store_out = pltpu.make_async_copy(out_v, out_hbm, out_sem.at[2])
    store_out.start()

    for way in range(2):
        @pl.when(open_way[way])
        def _(way=way):
            lr_copy(z, way).wait_send()
            for h in range(mine):
                for c in range(3):
                    tok_copy(z, c, h, way).wait_send()

    def drain(step, carry):
        for way in range(2):
            b = z - step if way == 0 else z + step
            arrives = from_left(step) if way == 0 else from_right(step)

            @pl.when(jnp.logical_and(arrives, open_way[way]))
            def _(way=way, b=b):
                lr_copy(b, way).wait_send()
                for h in range(mine):
                    for c in range(3):
                        tok_copy(b, c, h, way).wait_send()

            @pl.when(arrives)
            def _(way=way, b=b):
                for p in range(cuts * mine):
                    sum_copy(b, p, 1 - way).wait_send()

        return carry

    lax.fori_loop(1, n, drain, 0)
    for which in range(3):
        pair_copy(which).wait_send()
    store_own.wait()
    store_other.wait()
    store_out.wait()


def fused_device(queries, key_vectors, values, learn_rates, fast_weights, momentum):
    n = lax.axis_size("ctx")
    tokens = queries.shape[0]
    heads, _, rows, width = fast_weights.shape
    mine = heads // 2
    cuts = 2
    bf16, f32 = jnp.bfloat16, jnp.float32
    hbm = pl.BlockSpec(memory_space=pl.ANY)
    dma = pltpu.SemaphoreType.DMA
    vmem = pltpu.VMEM
    results = pl.pallas_call(
        functools.partial(fused_kernel, n, mine, momentum_decay, float(tokens * n) ** (-0.5)),
        out_shape=(
            jax.ShapeDtypeStruct((tokens, mine * width), bf16),
            jax.ShapeDtypeStruct(fast_weights.shape, f32),
        ),
        in_specs=[hbm, hbm, hbm, pl.BlockSpec(memory_space=pltpu.VMEM), hbm, hbm],
        out_specs=(hbm, hbm),
        scratch_shapes=[
            vmem((n, 3, mine, tokens, width), bf16),
            vmem((n, heads, 1, tokens), f32),
            vmem(fast_weights.shape, f32),
            vmem(fast_weights.shape, f32),
            vmem((mine, 3, 2 * rows, width), bf16),
            vmem((mine, 3, rows, width), bf16),
            vmem((mine, 3, rows, width), f32),
            vmem((mine, 3, rows, width), f32),
            vmem((mine, 3, 2 * rows, width), f32),
            vmem((mine, 3, 2 * rows, width), bf16),
            vmem((mine, 3, rows, width), bf16),
            vmem((mine, 3, rows, width), bf16),
            vmem((mine, tokens, width), f32),
            vmem((n, cuts * mine, tokens // cuts, width), bf16),
            vmem((n, cuts * mine, tokens // cuts, width), bf16),
            vmem((n, cuts * mine, tokens // cuts, width), bf16),
            vmem((tokens, mine * width), bf16),
            dma((4, max(mine, 2))),
            dma((2, n, 3, mine)),
            dma((n, 3, mine)),
            dma((2, n)),
            dma((n,)),
            dma((3,)),
            dma((3,)),
            dma((n, cuts * mine)),
            dma((2, n, cuts * mine)),
            dma((3,)),
        ],
        compiler_params=pltpu.CompilerParams(
            collective_id=0, has_side_effects=True, vmem_limit_bytes=56 * 1024 * 1024
        ),
    )(queries, key_vectors, values, learn_rates, fast_weights, momentum)
    layer_output, fast_updated = results
    return hand_over(layer_output, fast_updated)


def hand_over_kernel(out_in, fast_in, out_ref, fast_ref, out_v, fast_v, sem):
    count = fast_in.shape[0]
    reads = [pltpu.make_async_copy(out_in, out_v, sem.at[0])]
    writes = [pltpu.make_async_copy(out_v, out_ref, sem.at[0])]
    for i in range(count):
        reads.append(pltpu.make_async_copy(fast_in.at[i], fast_v.at[i], sem.at[1 + i]))
        writes.append(pltpu.make_async_copy(fast_v.at[i], fast_ref.at[i], sem.at[1 + i]))
    for read in reads:
        read.start()
    for read, write in zip(reads, writes):
        read.wait()
        write.start()
    for write in writes:
        write.wait()


def hand_over(layer_output, fast_updated):
    hbm = pl.BlockSpec(memory_space=pl.ANY)
    return pl.pallas_call(
        hand_over_kernel,
        out_shape=(
            jax.ShapeDtypeStruct(layer_output.shape, layer_output.dtype),
            jax.ShapeDtypeStruct(fast_updated.shape, fast_updated.dtype),
        ),
        in_specs=[hbm, hbm],
        out_specs=(hbm, hbm),
        scratch_shapes=[
            pltpu.VMEM(layer_output.shape, layer_output.dtype),
            pltpu.VMEM(fast_updated.shape, fast_updated.dtype),
            pltpu.SemaphoreType.DMA((1 + fast_updated.shape[0],)),
        ],
        compiler_params=pltpu.CompilerParams(vmem_limit_bytes=56 * 1024 * 1024),
    )(layer_output, fast_updated)


def per_device(*operands):
    queries, fast_weights = operands[0], operands[4]
    heads, _, rows, width = fast_weights.shape
    fits = lax.axis_size("rep") == 2 and heads % 2 == 0 and lax.axis_size("ctx") <= 4
    aligned = rows % 16 == 0 and width % 128 == 0 and queries.shape[0] == 128
    return (fused_device if fits and aligned else on_device)(*operands)


def solution(mesh):
    return jax.shard_map(
        per_device,
        mesh=mesh,
        in_specs=(
            P(("groups", "ctx"), "head"),
            P(("groups", "ctx"), "head"),
            P(("groups", "ctx"), "head"),
            P("head", ("groups", "ctx")),
            P(("groups", "head"), None, ("ctx", "rep"), None),
            P(("groups", "head"), None, ("ctx", "rep"), None),
        ),
        out_specs=(
            P(("groups", "ctx"), ("head", "rep")),
            P(("groups", "head"), None, ("ctx", "rep"), None),
        ),
        check_vma=False,
    )
```

```python
import functools

import jax
import jax.numpy as jnp
from jax import lax
from jax.experimental import pallas as pl
from jax.experimental.pallas import tpu as pltpu
from jax.sharding import PartitionSpec as P

epsilon = 1e-06
momentum_decay = 0.9


def passed_along(value, axis, steps):
    count = lax.axis_size(axis)
    initial, last = (max(0, -steps), min(count, count - steps))
    return lax.ppermute(value, axis, [(source, source + steps) for source in range(initial, last)])


def unit_rows(tensor):
    widened = tensor.astype(jnp.float32)
    factor = lax.rsqrt(jnp.mean(widened * widened, axis=-1, keepdims=True) + epsilon)
    return (widened * factor).astype(jnp.bfloat16)


def swiglu_apply(inputs, weights):
    gate = jnp.einsum("thd,hrd->htr", inputs, weights[:, 0], preferred_element_type=jnp.float32)
    upward = jnp.einsum("thd,hrd->htr", inputs, weights[:, 1], preferred_element_type=jnp.float32)
    hidden = (jax.nn.silu(gate) * upward).astype(jnp.bfloat16)
    return jnp.einsum("htr,hrd->htd", hidden, weights[:, 2], preferred_element_type=jnp.float32)


def window_attention(query_own, key_own, value_own, key_prior, value_prior, first_block):
    tok_rows = query_own.shape[0]
    per_rep = query_own.shape[1]
    width = query_own.shape[2]
    block_rows = min(tok_rows, 512)
    block_count = tok_rows // block_rows
    key_window = jnp.concatenate([key_prior, key_own], axis=0)
    value_window = jnp.concatenate([value_prior, value_own], axis=0)
    score_scale = width ** (-0.5)
    position = jnp.arange(2 * tok_rows)
    valid = jnp.logical_or(position >= tok_rows, jnp.logical_not(first_block))
    query_blocks = query_own.reshape(block_count, block_rows, per_rep, width)

    def one_block(query_block):
        scores = (
            jnp.einsum("tad,sad->ats", query_block, key_window, preferred_element_type=jnp.float32)
            * score_scale
        )
        scores = jnp.where(valid[None, None, :], scores, -jnp.inf)
        peak = jnp.max(scores, axis=-1, keepdims=True)
        weights = jnp.exp(scores - peak)
        probs = (weights / jnp.sum(weights, axis=-1, keepdims=True)).astype(jnp.bfloat16)
        return jnp.einsum("ats,sad->tad", probs, value_window, preferred_element_type=jnp.float32)

    return lax.map(one_block, query_blocks).reshape(tok_rows, per_rep, width)


def on_device(queries, key_vectors, values, learn_rates, fast_weights, momentum):
    tok_rows = queries.shape[0]
    head_count = fast_weights.shape[0]
    width = fast_weights.shape[3]
    rep_count = lax.axis_size("rep")
    per_rep = head_count // rep_count
    rep_index = lax.axis_index("rep")
    ctx_index = lax.axis_index("ctx")
    total_tokens = tok_rows * lax.axis_size("ctx")
    query_heads = queries.reshape(tok_rows, head_count, width)
    key_heads = key_vectors.reshape(tok_rows, head_count, width)
    value_heads = values.reshape(tok_rows, head_count, width)
    query_unit = unit_rows(query_heads)
    key_unit = unit_rows(key_heads)
    token_scale = float(total_tokens) ** (-0.5)
    cotangent = (
        -(learn_rates.T[:, :, None] * token_scale) * value_heads.astype(jnp.float32)
    ).astype(jnp.bfloat16)
    weight_rows = lax.all_gather(fast_weights.astype(jnp.bfloat16), "ctx", axis=2, tiled=True)
    gate = jnp.einsum(
        "thd,hrd->htr", key_unit, weight_rows[:, 0], preferred_element_type=jnp.float32
    )
    upward = jnp.einsum(
        "thd,hrd->htr", key_unit, weight_rows[:, 1], preferred_element_type=jnp.float32
    )
    back = jnp.einsum(
        "thd,hrd->htr", cotangent, weight_rows[:, 2], preferred_element_type=jnp.float32
    )
    sigma = jax.nn.sigmoid(gate)
    activated = jax.nn.silu(gate)
    hidden = (activated * upward).astype(jnp.bfloat16)
    gate_back = (back * upward * sigma * (1.0 + gate * (1.0 - sigma))).astype(jnp.bfloat16)
    up_back = (back * activated).astype(jnp.bfloat16)
    grad_gate = jnp.einsum("htr,thd->hrd", gate_back, key_unit, preferred_element_type=jnp.float32)
    grad_up = jnp.einsum("htr,thd->hrd", up_back, key_unit, preferred_element_type=jnp.float32)
    grad_down = jnp.einsum("htr,thd->hrd", hidden, cotangent, preferred_element_type=jnp.float32)
    gradient = jnp.stack([grad_gate, grad_up, grad_down], axis=1)
    share = lax.psum_scatter(
        gradient.astype(jnp.bfloat16), "ctx", scatter_dimension=2, tiled=True
    ).astype(jnp.float32)
    fast_updated = fast_weights - (momentum_decay * momentum + share)
    new_rows = lax.all_gather(fast_updated.astype(jnp.bfloat16), "ctx", axis=2, tiled=True)
    own_start = rep_index * per_rep
    partial_out = swiglu_apply(query_unit, new_rows)
    traded = lax.all_to_all(
        partial_out.astype(jnp.bfloat16), "rep", split_axis=0, concat_axis=0, tiled=True
    ).astype(partial_out.dtype)
    fast_out = jnp.sum(traded.reshape(rep_count, per_rep, tok_rows, width), axis=0)
    attend_query = lax.dynamic_slice_in_dim(query_heads, own_start, per_rep, 1)
    attend_key = lax.dynamic_slice_in_dim(key_heads, own_start, per_rep, 1)
    attend_value = lax.dynamic_slice_in_dim(value_heads, own_start, per_rep, 1)
    key_prior, value_prior = passed_along((attend_key, attend_value), "ctx", 1)
    attended = window_attention(
        attend_query, attend_key, attend_value, key_prior, value_prior, ctx_index == 0
    )
    combined = attended + jnp.transpose(fast_out, (1, 0, 2))
    layer_output = combined.astype(jnp.bfloat16).reshape(tok_rows, per_rep * width)
    return (layer_output, fast_updated)


def contract(left, right, left_dim, right_dim):
    return lax.dot_general(
        left, right, (((left_dim,), (right_dim,)), ((), ())), preferred_element_type=jnp.float32
    )


def fused_kernel(
    n, mine, decay, token_scale,
    q_hbm, k_hbm, v_hbm, lr_ref, fw_hbm, mom_hbm,
    out_hbm, fast_hbm,
    tok, lrs, fw, mom, weights, w_send, base_peer, base_send, grad, new_w, g_send, g_recv,
    attn, part, sums_right, sums_left, out_v,
    in_sem, tok_send, tok_recv, lr_send, lr_recv, pair_send, pair_recv, sum_send, sum_recv, out_sem,
):
    MESH = pl.DeviceIdType.MESH
    z = lax.axis_index("ctx")
    r = lax.axis_index("rep")
    heads, _, rows, width = fw.shape
    piece = part.shape[2]
    cuts = tok.shape[3] // piece
    has_left, has_right = z > 0, z < n - 1
    own, other = r * mine, (1 - r) * mine

    def load(c, h):
        ref = (k_hbm, v_hbm, q_hbm)[c]
        column = pl.multiple_of((own + h) * width, 128)
        return pltpu.make_async_copy(ref.at[:, pl.ds(column, width)], tok.at[z, c, h], in_sem.at[c, h])

    for c in range(3):
        for h in range(mine):
            load(c, h).start()
    load_fw = pltpu.make_async_copy(fw_hbm, fw, in_sem.at[3, 0])
    load_mom = pltpu.make_async_copy(mom_hbm, mom, in_sem.at[3, 1])
    load_fw.start()
    load_mom.start()
    for i in range(heads):
        lrs[z, i] = lr_ref[i : i + 1, :] * (-token_scale)

    barrier = pltpu.get_barrier_semaphore()
    pl.semaphore_signal(barrier, inc=1, device_id={"rep": 1 - r}, device_id_type=MESH)

    @pl.when(has_left)
    def _():
        pl.semaphore_signal(barrier, inc=1, device_id={"ctx": z - 1}, device_id_type=MESH)

    @pl.when(has_right)
    def _():
        pl.semaphore_signal(barrier, inc=1, device_id={"ctx": z + 1}, device_id_type=MESH)

    pl.semaphore_wait(barrier, 1 + has_left.astype(jnp.int32) + has_right.astype(jnp.int32))

    def tok_copy(b, c, h, way):
        return pltpu.make_async_remote_copy(
            src_ref=tok.at[b, c, h], dst_ref=tok.at[b, c, h],
            send_sem=tok_send.at[way, b, c, h], recv_sem=tok_recv.at[b, c, h],
            device_id={"ctx": z + 1 - 2 * way}, device_id_type=MESH,
        )

    def lr_copy(b, way):
        return pltpu.make_async_remote_copy(
            src_ref=lrs.at[b], dst_ref=lrs.at[b],
            send_sem=lr_send.at[way, b], recv_sem=lr_recv.at[b],
            device_id={"ctx": z + 1 - 2 * way}, device_id_type=MESH,
        )

    def pair_copy(which):
        src, dst = (
            (w_send, weights.at[:, :, pl.ds(rows, rows), :]),
            (base_send, base_peer),
            (g_send, g_recv),
        )[which]
        return pltpu.make_async_remote_copy(
            src_ref=src, dst_ref=dst, send_sem=pair_send.at[which], recv_sem=pair_recv.at[which],
            device_id={"rep": 1 - r}, device_id_type=MESH,
        )

    def sum_copy(b, h, way):
        return pltpu.make_async_remote_copy(
            src_ref=part.at[b, h], dst_ref=(sums_right, sums_left)[way].at[b, h],
            send_sem=sum_send.at[b, h], recv_sem=sum_recv.at[way, b, h],
            device_id={"ctx": z + 1 - 2 * way}, device_id_type=MESH,
        )

    open_way = (has_right, has_left)

    def own_send(make):
        for way in range(2):
            pl.when(open_way[way])(lambda way=way: make(way).start())

    own_send(lambda way: lr_copy(z, way))
    for h in range(mine):
        for c in range(2):
            load(c, h).wait()
            own_send(lambda way: tok_copy(z, c, h, way))
    for h in range(mine):
        load(2, h).wait()

    def own_queries(step):
        for way in range(2):
            last = z if way == 0 else n - 1 - z

            @pl.when(jnp.logical_and(step == last, open_way[way]))
            def _(way=way):
                for h in range(mine):
                    tok_copy(z, 2, h, way).start()

    own_queries(0)

    load_fw.wait()
    for h in range(mine):
        for m in range(3):
            w_send[h, m] = fw[other + h, m].astype(jnp.bfloat16)
    pair_copy(0).start()
    for h in range(mine):
        for m in range(3):
            weights[h, m, :rows] = fw[own + h, m].astype(jnp.bfloat16)
    load_mom.wait()
    for h in range(mine):
        for m in range(3):
            base_send[h, m] = fw[other + h, m] - decay * mom[other + h, m]
    pair_copy(1).start()
    pair_copy(0).wait_recv()

    def grad_block(b, first):
        @pl.loop(0, mine)
        def _(h):
            key = unit_rows(tok[b, 0, h])
            value = tok[b, 1, h]
            rate = lrs[b, own + h]
            both = contract(weights[h, 0:2].reshape(4 * rows, width), key, 1, 1)
            gate, upward = both[: 2 * rows], both[2 * rows :]
            back = contract(weights[h, 2], value, 1, 1) * rate
            sigma = jax.nn.sigmoid(gate)
            activated = gate * sigma
            hidden = (activated * upward * rate).astype(jnp.bfloat16)
            gate_back = (back * upward * sigma * (1.0 + gate * (1.0 - sigma))).astype(jnp.bfloat16)
            up_back = (back * activated).astype(jnp.bfloat16)
            terms = (
                contract(gate_back, key, 1, 0),
                contract(up_back, key, 1, 0),
                contract(hidden, value, 1, 0),
            )
            for m in range(3):
                grad[h, m] = terms[m] if first else grad[h, m] + terms[m]

    def attend(with_prior):
        @pl.loop(0, mine)
        def _(h):
            query = tok[z, 2, h]
            scale = width ** (-0.5)
            scores = contract(query, tok[z, 0, h], 1, 1) * scale
            peak = jnp.max(scores, axis=-1, keepdims=True)
            if with_prior:
                prior = contract(query, tok[z - 1, 0, h], 1, 1) * scale
                peak = jnp.maximum(peak, jnp.max(prior, axis=-1, keepdims=True))
                prior = jnp.exp(prior - peak)
            scores = jnp.exp(scores - peak)
            total = jnp.sum(scores, axis=-1, keepdims=True)
            if with_prior:
                total = total + jnp.sum(prior, axis=-1, keepdims=True)
            result = contract((scores / total).astype(jnp.bfloat16), tok[z, 1, h], 1, 0)
            if with_prior:
                result = result + contract((prior / total).astype(jnp.bfloat16), tok[z - 1, 1, h], 1, 0)
            attn[h] = result

    def from_left(step):
        return z - step >= 0

    def from_right(step):
        return z + step < n

    grad_block(z, True)

    @pl.when(z == 0)
    def _():
        attend(False)

    def pass_on(step, pieces, with_lr):
        arrives = (from_left(step), from_right(step))
        for way in range(2):
            b = z - step if way == 0 else z + step
            if with_lr:
                @pl.when(arrives[way])
                def _(way=way, b=b):
                    lr_copy(b, way).wait_recv()
                    pl.when(open_way[way])(lambda: lr_copy(b, way).start())

        for c, h in pieces:
            for way in range(2):
                b = z - step if way == 0 else z + step

                @pl.when(arrives[way])
                def _(way=way, b=b):
                    tok_copy(b, c, h, way).wait_recv()
                    pl.when(open_way[way])(lambda: tok_copy(b, c, h, way).start())

    def keys_step(step, carry):
        pass_on(step, [(c, h) for h in range(mine) for c in range(2)], True)

        @pl.when(from_left(step))
        def _():
            grad_block(z - step, False)

        @pl.when(from_right(step))
        def _():
            grad_block(z + step, False)

        @pl.when(jnp.logical_and(step == 1, has_left))
        def _():
            attend(True)

        return carry

    lax.fori_loop(1, n, keys_step, 0)

    pair_copy(1).wait_recv()
    for h in range(mine):
        for m in range(3):
            fresh = fw[own + h, m] - (decay * mom[own + h, m] + grad[h, m, :rows])
            fw[own + h, m] = fresh
            new_w[h, m, :rows] = fresh.astype(jnp.bfloat16)
            new_w[h, m, rows:] = (base_peer[h, m] - grad[h, m, rows:]).astype(jnp.bfloat16)
            g_send[h, m] = grad[h, m, rows:].astype(jnp.bfloat16)
    pair_copy(2).start()
    store_own = pltpu.make_async_copy(
        fw.at[pl.ds(own, mine)], fast_hbm.at[pl.ds(own, mine)], out_sem.at[0]
    )
    store_own.start()

    def apply(b, h):
        query = unit_rows(tok[b, 2, h])
        gate = contract(query, new_w[h, 0], 1, 1)
        upward = contract(query, new_w[h, 1], 1, 1)
        hidden = (gate * jax.nn.sigmoid(gate) * upward).astype(jnp.bfloat16)
        return contract(hidden, new_w[h, 2], 1, 0)

    @pl.loop(0, mine)
    def _(h):
        attn[h] = attn[h] + apply(z, h)

    near_left = 2 * z < n - 1

    def queries_step(step, carry):
        for h in range(mine):
            for way, when in ((0, near_left), (1, None), (0, jnp.logical_not(near_left))):
                b = step if way == 0 else n - 1 - step
                there = b < z if way == 0 else b > z

                @pl.when(there if when is None else jnp.logical_and(there, when))
                def _(b=b, way=way):
                    tok_copy(b, 2, h, way).wait_recv()
                    pl.when(open_way[way])(lambda: tok_copy(b, 2, h, way).start())
                    result = apply(b, h).astype(jnp.bfloat16)
                    for half in range(cuts):
                        part[b, cuts * h + half] = result[half * piece : (half + 1) * piece]

                    @pl.when(jnp.logical_not(open_way[way]))
                    def _():
                        for half in range(cuts):
                            sum_copy(b, cuts * h + half, 1 - way).start()

            for way in range(2):
                last = z - 1 if way == 0 else n - 2 - z

                @pl.when(jnp.logical_and(step == last, open_way[way]))
                def _(way=way):
                    tok_copy(z, 2, h, way).start()

        return carry

    lax.fori_loop(0, n - 1, queries_step, 0)

    def merge_step(turn, carry):
        step = n - turn
        for h in range(cuts * mine):
            for way, when in ((0, near_left), (1, None), (0, jnp.logical_not(near_left))):
                b = step if way == 0 else n - 1 - step
                there = jnp.logical_and(b > z, has_left) if way == 0 else jnp.logical_and(b < z, has_right)

                @pl.when(there if when is None else jnp.logical_and(there, when))
                def _(b=b, way=way):
                    sum_copy(b, h, way).wait_recv()
                    arrived = (sums_right, sums_left)[way][b, h].astype(jnp.float32)
                    part[b, h] = (part[b, h].astype(jnp.float32) + arrived).astype(jnp.bfloat16)
                    sum_copy(b, h, way).start()

        return carry

    lax.fori_loop(1, n, merge_step, 0)

    pair_copy(2).wait_recv()
    for h in range(mine):
        for m in range(3):
            fw[other + h, m] = fw[other + h, m] - (
                decay * mom[other + h, m] + g_recv[h, m].astype(jnp.float32)
            )
    store_other = pltpu.make_async_copy(
        fw.at[pl.ds(other, mine)], fast_hbm.at[pl.ds(other, mine)], out_sem.at[1]
    )
    store_other.start()

    for p in range(cuts * mine):
        h, at = p // cuts, pl.ds(p % cuts * piece, piece)

        @pl.when(has_left)
        def _():
            sum_copy(z, p, 0).wait_recv()
            attn[h, at] = attn[h, at] + sums_right[z, p].astype(jnp.float32)

        @pl.when(has_right)
        def _():
            sum_copy(z, p, 1).wait_recv()
            attn[h, at] = attn[h, at] + sums_left[z, p].astype(jnp.float32)

        out_v[at, h * width : (h + 1) * width] = attn[h, at].astype(jnp.bfloat16)
    store_out = pltpu.make_async_copy(out_v, out_hbm, out_sem.at[2])
    store_out.start()

    for way in range(2):
        @pl.when(open_way[way])
        def _(way=way):
            lr_copy(z, way).wait_send()
            for h in range(mine):
                for c in range(3):
                    tok_copy(z, c, h, way).wait_send()

    def drain(step, carry):
        for way in range(2):
            b = z - step if way == 0 else z + step
            arrives = from_left(step) if way == 0 else from_right(step)

            @pl.when(jnp.logical_and(arrives, open_way[way]))
            def _(way=way, b=b):
                lr_copy(b, way).wait_send()
                for h in range(mine):
                    for c in range(3):
                        tok_copy(b, c, h, way).wait_send()

            @pl.when(arrives)
            def _(way=way, b=b):
                for p in range(cuts * mine):
                    sum_copy(b, p, 1 - way).wait_send()

        return carry

    lax.fori_loop(1, n, drain, 0)
    for which in range(3):
        pair_copy(which).wait_send()
    store_own.wait()
    store_other.wait()
    store_out.wait()


def fused_device(queries, key_vectors, values, learn_rates, fast_weights, momentum):
    n = lax.axis_size("ctx")
    tokens = queries.shape[0]
    heads, _, rows, width = fast_weights.shape
    mine = heads // 2
    cuts = 2
    bf16, f32 = jnp.bfloat16, jnp.float32
    hbm = pl.BlockSpec(memory_space=pl.ANY)
    dma = pltpu.SemaphoreType.DMA
    vmem = pltpu.VMEM
    results = pl.pallas_call(
        functools.partial(fused_kernel, n, mine, momentum_decay, float(tokens * n) ** (-0.5)),
        out_shape=(
            jax.ShapeDtypeStruct((tokens, mine * width), bf16),
            jax.ShapeDtypeStruct(fast_weights.shape, f32),
        ),
        in_specs=[hbm, hbm, hbm, pl.BlockSpec(memory_space=pltpu.VMEM), hbm, hbm],
        out_specs=(hbm, hbm),
        scratch_shapes=[
            vmem((n, 3, mine, tokens, width), bf16),
            vmem((n, heads, 1, tokens), f32),
            vmem(fast_weights.shape, f32),
            vmem(fast_weights.shape, f32),
            vmem((mine, 3, 2 * rows, width), bf16),
            vmem((mine, 3, rows, width), bf16),
            vmem((mine, 3, rows, width), f32),
            vmem((mine, 3, rows, width), f32),
            vmem((mine, 3, 2 * rows, width), f32),
            vmem((mine, 3, 2 * rows, width), bf16),
            vmem((mine, 3, rows, width), bf16),
            vmem((mine, 3, rows, width), bf16),
            vmem((mine, tokens, width), f32),
            vmem((n, cuts * mine, tokens // cuts, width), bf16),
            vmem((n, cuts * mine, tokens // cuts, width), bf16),
            vmem((n, cuts * mine, tokens // cuts, width), bf16),
            vmem((tokens, mine * width), bf16),
            dma((4, max(mine, 2))),
            dma((2, n, 3, mine)),
            dma((n, 3, mine)),
            dma((2, n)),
            dma((n,)),
            dma((3,)),
            dma((3,)),
            dma((n, cuts * mine)),
            dma((2, n, cuts * mine)),
            dma((3,)),
        ],
        compiler_params=pltpu.CompilerParams(
            collective_id=0, has_side_effects=True, vmem_limit_bytes=56 * 1024 * 1024
        ),
    )(queries, key_vectors, values, learn_rates, fast_weights, momentum)
    layer_output, fast_updated = results
    return hand_over(layer_output, fast_updated)


def hand_over_kernel(out_in, fast_in, out_ref, fast_ref, out_v, fast_v, sem):
    count = fast_in.shape[0]
    reads = [pltpu.make_async_copy(out_in, out_v, sem.at[0])]
    writes = [pltpu.make_async_copy(out_v, out_ref, sem.at[0])]
    for i in range(count):
        reads.append(pltpu.make_async_copy(fast_in.at[i], fast_v.at[i], sem.at[1 + i]))
        writes.append(pltpu.make_async_copy(fast_v.at[i], fast_ref.at[i], sem.at[1 + i]))
    for read in reads:
        read.start()
    for read, write in zip(reads, writes):
        read.wait()
        write.start()
    for write in writes:
        write.wait()


def hand_over(layer_output, fast_updated):
    hbm = pl.BlockSpec(memory_space=pl.ANY)
    return pl.pallas_call(
        hand_over_kernel,
        out_shape=(
            jax.ShapeDtypeStruct(layer_output.shape, layer_output.dtype),
            jax.ShapeDtypeStruct(fast_updated.shape, fast_updated.dtype),
        ),
        in_specs=[hbm, hbm],
        out_specs=(hbm, hbm),
        scratch_shapes=[
            pltpu.VMEM(layer_output.shape, layer_output.dtype),
            pltpu.VMEM(fast_updated.shape, fast_updated.dtype),
            pltpu.SemaphoreType.DMA((1 + fast_updated.shape[0],)),
        ],
        compiler_params=pltpu.CompilerParams(vmem_limit_bytes=56 * 1024 * 1024),
    )(layer_output, fast_updated)


def per_device(*operands):
    queries, fast_weights = operands[0], operands[4]
    heads, _, rows, width = fast_weights.shape
    fits = lax.axis_size("rep") == 2 and heads % 2 == 0 and lax.axis_size("ctx") <= 4
    aligned = rows % 16 == 0 and width % 128 == 0 and queries.shape[0] == 128
    return (fused_device if fits and aligned else on_device)(*operands)


def solution(mesh):
    return jax.shard_map(
        per_device,
        mesh=mesh,
        in_specs=(
            P(("groups", "ctx"), "head"),
            P(("groups", "ctx"), "head"),
            P(("groups", "ctx"), "head"),
            P("head", ("groups", "ctx")),
            P(("groups", "head"), None, ("ctx", "rep"), None),
            P(("groups", "head"), None, ("ctx", "rep"), None),
        ),
        out_specs=(
            P(("groups", "ctx"), ("head", "rep")),
            P(("groups", "head"), None, ("ctx", "rep"), None),
        ),
        check_vma=False,
    )
```
